32 devices in a mesh: fsdp: 4 (over y, x), ctx: 8 (over z, core).
Axes of the slice: x: 2, y: 2, z: 4, core: 2. Of those that a mesh axis runs over, the one named last changes fastest.
Arguments:
- hidden_in: bfloat16 [2, 8192, 2048], P(None, ('fsdp', 'ctx')), may hold values from -6 to 6
- segment_ids: int32 [2, 8192], P(None, ('fsdp', 'ctx')), may hold values from 0 to 2, as said below
- positions: int32 [2, 8192], P(None, ('fsdp', 'ctx')), may hold values from 0 to 1535, as said below
- norm1_gain: bfloat16 [2048], P('fsdp'), may hold values from 0.5 to 1.5
- norm1_bias: bfloat16 [2048], P('fsdp'), may hold values from -3 to 3
- query_weight: bfloat16 [2048, 2048], P('fsdp'), may hold values from -0.125 to 0.125
- query_bias: bfloat16 [2048], P('fsdp'), may hold values from -4 to 4
- keyval_weight: bfloat16 [2048, 256], P('fsdp'), may hold values from -0.125 to 0.125
- value_bias: bfloat16 [128], P('fsdp'), may hold values from -0.75 to 0.75
- out_weight: bfloat16 [2048, 2048], P('fsdp'), may hold values from -1.5 to 1.5
- out_bias: bfloat16 [2048], P('fsdp'), may hold values from -3 to 3
- norm2_gain: bfloat16 [2048], P('fsdp'), may hold values from 0.5 to 1.5
- norm2_bias: bfloat16 [2048], P('fsdp'), may hold values from -3 to 3
- fc_weight: bfloat16 [2048, 8192], P('fsdp'), may hold values from -0.125 to 0.125
- fc_bias: bfloat16 [8192], P('fsdp'), may hold values from -4 to 4
- proj_weight: bfloat16 [8192, 2048], P('fsdp'), may hold values from -0.0625 to 0.0625
- proj_bias: bfloat16 [2048], P('fsdp'), may hold values from -3 to 3
- out_grad: bfloat16 [2, 8192, 2048], P(None, ('fsdp', 'ctx')), may hold values from -6 to 6
Outputs:
- hidden_out: bfloat16 [2, 8192, 2048], P(None, ('fsdp', 'ctx'))
- hidden_grad: float32 [2, 8192, 2048], P(None, ('fsdp', 'ctx'))
- norm1_gain_grad: float32 [2048], P('fsdp')
- norm1_bias_grad: float32 [2048], P('fsdp')
- query_weight_grad: float32 [2048, 2048], P('fsdp')
- query_bias_grad: float32 [2048], P('fsdp')
- keyval_weight_grad: float32 [2048, 256], P('fsdp')
- value_bias_grad: float32 [128], P('fsdp')
- out_weight_grad: float32 [2048, 2048], P('fsdp')
- out_bias_grad: float32 [2048], P('fsdp')
- norm2_gain_grad: float32 [2048], P('fsdp')
- norm2_bias_grad: float32 [2048], P('fsdp')
- fc_weight_grad: float32 [2048, 8192], P('fsdp')
- fc_bias_grad: float32 [8192], P('fsdp')
- proj_weight_grad: float32 [8192, 2048], P('fsdp')
- proj_bias_grad: float32 [2048], P('fsdp')
The draws below stay inside these ranges and needn't reach their ends.
Inputs may be any that keep to these rules, and one draw needn't show every extreme that they name: `segment_ids`: in each group of 2048 consecutive tokens of a micro-batch, segment 0 holds positions 0 to 1023 once each and each segment k of 1 to 2 holds positions 1024 to 1535 once each. Tokens come in aligned runs of 64 consecutive positions of one segment; a group's first run is positions 0 to 63 of the prompt and its last run is the prompt's last 64 positions; the other runs are in any order. `positions`: as stated for segment_ids.
All inputs are finite; a program needn't handle non-finite values.
Results may differ from the reference program's by a relative error of at most 0.015.
Values may be sent and summed in bfloat16 or wider, within the bound.
A program may use at most 448 MiB of HBM per device.

```python
import math
import jax
import jax.numpy as jnp
from jax import lax

D = 2048
HEADS = 16
HD = 128
FF = 8192
PROMPT = 1024
CONT = 512
CONTS = 2
MICRO = 2
BLOCK = 64
GROUP = 2048
TOKENS = 8192


def token_layout(key):
    groups = MICRO * (TOKENS // GROUP)
    prompt_runs = PROMPT // BLOCK
    cont_runs = CONT // BLOCK
    run_count = prompt_runs + CONTS * cont_runs
    run_segment = jnp.concatenate([jnp.zeros((prompt_runs,), jnp.int32), jnp.repeat(jnp.arange(1, CONTS + 1, dtype=jnp.int32), cont_runs)])
    run_first = jnp.concatenate([jnp.arange(prompt_runs, dtype=jnp.int32) * BLOCK, PROMPT + jnp.tile(jnp.arange(cont_runs, dtype=jnp.int32) * BLOCK, CONTS)])
    movable = jnp.concatenate([jnp.arange(1, prompt_runs - 1, dtype=jnp.int32), jnp.arange(prompt_runs, run_count, dtype=jnp.int32)])

    def one_group(group_key):
        shuffled = jax.random.permutation(group_key, movable)
        return jnp.concatenate([jnp.zeros((1,), jnp.int32), shuffled, jnp.full((1,), prompt_runs - 1, jnp.int32)])
    order = jax.vmap(one_group)(jax.random.split(key, groups))
    seg_tokens = jnp.repeat(run_segment[order], BLOCK, axis=1)
    offsets = jnp.arange(BLOCK, dtype=jnp.int32)
    pos_tokens = (run_first[order][:, :, None] + offsets[None, None, :]).reshape(groups, run_count * BLOCK)
    return (seg_tokens.reshape(MICRO, TOKENS), pos_tokens.reshape(MICRO, TOKENS))


def draw_segment_ids(key, part):
    shared = token_layout(key)
    return shared[0]


def draw_positions(key, part):
    shared = token_layout(key)
    return shared[1]


def with_spikes(drawn, rng, source, target, shards_of, factor):
    owner, partner = [(jnp.arange(drawn.shape[position]) // (drawn.shape[position] // shards_of)).reshape([-1 if axis == position else 1 for axis in range(drawn.ndim)]) for position in (source, target)]
    chosen = jax.random.permutation(rng, shards_of)[partner]
    strong = (owner == chosen) | (owner == (partner + shards_of // 2) % shards_of)
    return jnp.where(strong, factor * drawn, drawn)


def levels(own_key, shape, cuts, smallest, top_value):
    def one(dim, parts):
        heights = jax.random.uniform(jax.random.fold_in(jax.random.fold_in(own_key, 6), dim), (parts,), jnp.float32, smallest / len(cuts), top_value / len(cuts))
        return jnp.repeat(jnp.exp(heights), shape[dim] // parts).reshape((-1,) + (1,) * (len(shape) - dim - 1))

    factor_of = one(*cuts[0])
    for cut in cuts[1:]:
        factor_of = factor_of * one(*cut)
    return factor_of


def bell_draw(rng, shape, deviation, bound, pieces=(), held_as=jnp.bfloat16):
    values = deviation * jax.random.normal(rng, shape, jnp.float32)
    if pieces:
        values = values * levels(rng, shape, pieces, -0.22, 0.18)
    return jnp.clip(values, -bound, bound).astype(held_as)


def bell_draw_with(stream_key, extent, scale, most, cuts, heavy, kind=jnp.bfloat16):
    values = scale * jax.random.normal(stream_key, extent, jnp.float32)
    if cuts:
        values = values * levels(stream_key, extent, cuts, -0.22, 0.18)
    return jnp.clip(with_spikes(values, jax.random.fold_in(stream_key, 3), *heavy), -most, most).astype(kind)


def setup_inputs(seed: int = 0) -> dict:
    streams_of = jax.random.split(jax.random.key(seed), 19)
    hidden_in = bell_draw(streams_of[0], (MICRO, TOKENS, D), 1.0, 6.0, ((1, 32),))
    segment_ids = draw_segment_ids(jax.random.fold_in(streams_of[18], 71), 0)
    positions = draw_positions(jax.random.fold_in(streams_of[18], 71), 0)
    norm1_gain = jnp.clip(1.0 + 0.1 * jax.random.normal(streams_of[3], (D,), jnp.float32), 0.5, 1.5).astype(jnp.bfloat16)
    norm1_bias = bell_draw(streams_of[4], (D,), 0.2, 3.0, ((0, 4),))
    query_weight = bell_draw(streams_of[5], (D, D), D ** -0.5, 0.125, ((0, 4),))
    query_bias = bell_draw(streams_of[6], (D,), 0.3, 4.0, ((0, 4),))
    keyval_weight = bell_draw(streams_of[7], (D, 2 * HD), D ** -0.5, 0.125, ((0, 4),))
    value_bias = bell_draw(streams_of[8], (HD,), 0.05, 0.75, ((0, 4),))
    out_weight = bell_draw(streams_of[9], (D, D), (D // 128) ** -0.5, 1.5, ((0, 4),))
    out_bias = bell_draw(streams_of[10], (D,), 0.2, 3.0, ((0, 4),))
    norm2_gain = jnp.clip(1.0 + 0.1 * jax.random.normal(streams_of[11], (D,), jnp.float32), 0.5, 1.5).astype(jnp.bfloat16)
    norm2_bias = bell_draw(streams_of[12], (D,), 0.2, 3.0, ((0, 4),))
    fc_weight = bell_draw(streams_of[13], (D, FF), D ** -0.5, 0.125, ((0, 4),))
    fc_bias = bell_draw(streams_of[14], (FF,), 0.3, 4.0, ((0, 4),))
    proj_weight = bell_draw(streams_of[15], (FF, D), FF ** -0.5, 0.0625, ((0, 4),))
    proj_bias = bell_draw(streams_of[16], (D,), 0.2, 3.0, ((0, 4),))
    out_grad = bell_draw_with(streams_of[17], (MICRO, TOKENS, D), 1.0, 6.0, ((1, 32),), (1, 2, 32, 2.75))
    return dict(hidden_in=hidden_in, segment_ids=segment_ids, positions=positions, norm1_gain=norm1_gain, norm1_bias=norm1_bias, query_weight=query_weight, query_bias=query_bias, keyval_weight=keyval_weight, value_bias=value_bias, out_weight=out_weight, out_bias=out_bias, norm2_gain=norm2_gain, norm2_bias=norm2_bias, fc_weight=fc_weight, fc_bias=fc_bias, proj_weight=proj_weight, proj_bias=proj_bias, out_grad=out_grad)


HIGH = lax.Precision.HIGHEST

@jax.custom_vjp
def low(v):
    return lax.optimization_barrier(v.astype(jnp.bfloat16)).astype(jnp.float32)

@jax.custom_vjp
def low_back(v):
    return v

def low_keep(v):
    return (low(v), None)

def low_pass(kept, grad):
    return (grad,)

def back_keep(v):
    return (v, None)

def back_low(kept, grad):
    return (low(grad),)
low.defvjp(low_keep, low_pass)
low_back.defvjp(back_keep, back_low)

def layer_norm(values, gain, shift):
    center = lax.optimization_barrier(jnp.mean(values, axis=-1, keepdims=True))
    shifted = values - center
    spread = lax.optimization_barrier(jnp.mean(shifted * shifted, axis=-1, keepdims=True))
    return shifted * lax.rsqrt(spread + 1e-05) * gain + shift

def attend_block(query_block, seg_here, pos_here, keys, values, seg_all, pos_all):
    scores = jnp.einsum('qhd,kd->hqk', query_block, keys, precision=HIGH) * (1.0 / math.sqrt(HD))
    scores = low_back(scores)
    visible = (pos_all[None, :] <= pos_here[:, None]) & ((seg_all[None, :] == 0) | (seg_all[None, :] == seg_here[:, None]))
    scores = jnp.where(visible[None], scores, -1e+30)
    peak = lax.optimization_barrier(jnp.max(scores, axis=-1, keepdims=True))
    expo = jnp.exp(scores - peak)
    probs = expo / lax.optimization_barrier(jnp.sum(expo, axis=-1, keepdims=True))
    mixed = jnp.einsum('hqk,kd->qhd', low(probs), values, precision=HIGH)
    return mixed.reshape(mixed.shape[0], HEADS * HD)

def group_forward(hidden, seg_ids, pos_ids, params):
    norm1_gain, norm1_bias, query_weight, query_bias, keyval_weight, value_bias, out_weight, out_bias, norm2_gain, norm2_bias, fc_weight, fc_bias, proj_weight, proj_bias = params
    normed = low(layer_norm(hidden, norm1_gain, norm1_bias))
    queries = low(low_back(jnp.dot(normed, query_weight, precision=HIGH) + query_bias))
    kv_bias = jnp.concatenate([jnp.zeros((HD,), value_bias.dtype), value_bias])
    keyvals = low(low_back(jnp.dot(normed, keyval_weight, precision=HIGH) + kv_bias))
    keys = keyvals[:, :HD]
    values = keyvals[:, HD:]
    block_rows = 512 if GROUP % 512 == 0 else GROUP
    block_count = GROUP // block_rows
    items = (queries.reshape(block_count, block_rows, HEADS, HD), seg_ids.reshape(block_count, block_rows), pos_ids.reshape(block_count, block_rows))

    def one_block(item):
        return jax.checkpoint(attend_block)(item[0], item[1], item[2], keys, values, seg_ids, pos_ids)
    mixed = lax.map(one_block, items).reshape(GROUP, HEADS * HD)
    mixed = low(low_back(mixed))
    middle = hidden + low_back(jnp.dot(mixed, out_weight, precision=HIGH) + out_bias)
    normed2 = low(layer_norm(middle, norm2_gain, norm2_bias))
    before = low_back(jnp.dot(normed2, fc_weight, precision=HIGH) + fc_bias)
    active = low(jax.nn.gelu(before, approximate=True))
    return middle + jnp.dot(active, proj_weight, precision=HIGH) + proj_bias

def reference(hidden_in, segment_ids, positions, norm1_gain, norm1_bias, query_weight, query_bias, keyval_weight, value_bias, out_weight, out_bias, norm2_gain, norm2_bias, fc_weight, fc_bias, proj_weight, proj_bias, out_grad):
    params = tuple((array.astype(jnp.float32) for array in (norm1_gain, norm1_bias, query_weight, query_bias, keyval_weight, value_bias, out_weight, out_bias, norm2_gain, norm2_bias, fc_weight, fc_bias, proj_weight, proj_bias)))
    groups = MICRO * (TOKENS // GROUP)
    inputs = hidden_in.astype(jnp.float32).reshape(groups, GROUP, D)
    seg_groups = segment_ids.reshape(groups, GROUP)
    pos_groups = positions.reshape(groups, GROUP)

    def forward(inputs, params):

        def one_group(item):
            return jax.checkpoint(group_forward)(item[0], item[1], item[2], params)
        return lax.map(one_group, (inputs, seg_groups, pos_groups))
    result, pullback = jax.vjp(forward, inputs, params)
    input_grad, grads = pullback(out_grad.astype(jnp.float32).reshape(groups, GROUP, D))
    return (result.reshape(MICRO, TOKENS, D).astype(jnp.bfloat16), input_grad.reshape(MICRO, TOKENS, D), grads[0], grads[1], grads[2], grads[3], grads[4], grads[5], grads[6], grads[7], grads[8], grads[9], grads[10], grads[11], grads[12], grads[13])
```

```python
import math

import jax
import jax.numpy as jnp
from jax import lax
from jax.sharding import PartitionSpec as P

D = 2048
HEADS = 16
HD = 128
QUAD = 4
F32 = jnp.float32
BF16 = jnp.bfloat16


def layer_norm(values, gain, shift):
    center = jnp.mean(values, axis=-1, keepdims=True)
    shifted = values - center
    spread = jnp.mean(shifted * shifted, axis=-1, keepdims=True)
    return shifted * lax.rsqrt(spread + 1e-05) * gain + shift


def layer_norm_back(values, gain, d_out):
    center = jnp.mean(values, axis=-1, keepdims=True)
    shifted = values - center
    spread = jnp.mean(shifted * shifted, axis=-1, keepdims=True)
    r = lax.rsqrt(spread + 1e-05)
    xhat = shifted * r
    e = d_out * gain
    d_values = r * (
        e - jnp.mean(e, axis=-1, keepdims=True) - xhat * jnp.mean(e * xhat, axis=-1, keepdims=True)
    )
    return d_values, jnp.sum(d_out * xhat, axis=0), jnp.sum(d_out, axis=0)


def gelu_and_slope(u):
    a = math.sqrt(2.0 / math.pi)
    t = jnp.tanh(a * (u + 0.044715 * u * u * u))
    half = 0.5 * (1.0 + t)
    slope = half + 0.5 * u * (1.0 - t * t) * a * (1.0 + 3.0 * 0.044715 * u * u)
    return u * half, slope


def dot(a, b):
    return jnp.dot(a, b, preferred_element_type=F32)


def dot_t(a, b):
    return lax.dot_general(a, b, (((1,), (1,)), ((), ())), preferred_element_type=F32)


def t_dot(a, b):
    return lax.dot_general(a, b, (((0,), (0,)), ((), ())), preferred_element_type=F32)


def swap_f(x, bit, size):
    return lax.ppermute(x, "fsdp", [(i, i ^ bit) for i in range(size)])


def swap_k(x, bit, size):
    return lax.ppermute(x, "ctx", [(i, i ^ bit) for i in range(size)])


def bits_of(size):
    out = []
    bit = 1
    while bit < size:
        out.append(bit)
        bit *= 2
    return out


def gather_f(piece, f, size):
    rows, n = piece.shape
    half = rows // 2
    orders = (bits_of(size), bits_of(size)[::-1])
    out = jnp.zeros((size, 2, half, n), piece.dtype)
    for h, order in enumerate(orders):
        held = {0: piece[h * half : (h + 1) * half]}
        for bit in order:
            for d in list(held):
                held[d ^ bit] = swap_f(held[d], bit, size)
        for d, part in held.items():
            out = lax.dynamic_update_slice(out, part[None, None], (f ^ d, h, 0, 0))
    return out.reshape(size * rows, n)


def reduce_f(term, size):
    outs = []
    for h, order in enumerate((bits_of(size), bits_of(size)[::-1])):
        sums = {d: (lambda d=d, h=h: term(d, h)) for d in range(size)}
        extra = {d: [] for d in range(size)}

        def value(d):
            total = sums[d]()
            for e in extra[d]:
                total = total + e.astype(F32)
            return total

        left = set(range(size))
        for bit in order:
            for d in sorted(left, reverse=True):
                if d & bit:
                    extra[d ^ bit].append(swap_f(value(d).astype(BF16), bit, size))
                    left.discard(d)
        outs.append(value(0))
    return jnp.concatenate(outs, axis=1)


def attend_forward(queries, keys, values, visible, head_block, scale):
    pieces = []
    lse_parts = []
    for start in range(0, HEADS, head_block):
        query_block = queries[:, start : start + head_block]
        scores = (
            jnp.einsum("qhd,kd->hqk", query_block, keys, preferred_element_type=F32) * scale
        )
        scores = jnp.where(visible[None], scores, -1e30)
        peak = jnp.max(scores, axis=-1, keepdims=True)
        expo = jnp.exp(scores - peak)
        total = jnp.sum(expo, axis=-1, keepdims=True)
        probs = expo / total
        lse_parts.append(peak[..., 0] + jnp.log(total[..., 0]))
        pieces.append(
            jnp.einsum("hqk,kd->qhd", probs.astype(BF16), values, preferred_element_type=F32)
        )
    return (jnp.concatenate(pieces, axis=1), jnp.concatenate(lse_parts, axis=0))


def attend_backward(queries, keys, values, visible, lse_rows, grad_mixed, head_block, scale):
    query_grads = []
    key_grad = jnp.zeros((keys.shape[0], HD), F32)
    value_grad = jnp.zeros((keys.shape[0], HD), F32)
    for start in range(0, HEADS, head_block):
        query_block = queries[:, start : start + head_block]
        grad_block = grad_mixed[:, start : start + head_block]
        scores = (
            jnp.einsum("qhd,kd->hqk", query_block, keys, preferred_element_type=F32) * scale
        )
        scores = jnp.where(visible[None], scores, -1e30)
        probs = jnp.exp(scores - lse_rows[start : start + head_block][..., None])
        grad_probs = jnp.einsum("qhd,kd->hqk", grad_block, values, preferred_element_type=F32)
        inner = jnp.sum(probs * grad_probs, axis=-1, keepdims=True)
        grad_scores = (probs * (grad_probs - inner)).astype(BF16)
        query_grads.append(
            jnp.einsum("hqk,kd->qhd", grad_scores, keys, preferred_element_type=F32) * scale
        )
        key_grad = (
            key_grad
            + jnp.einsum("hqk,qhd->kd", grad_scores, query_block, preferred_element_type=F32)
            * scale
        )
        value_grad = value_grad + jnp.einsum(
            "hqk,qhd->kd", probs.astype(BF16), grad_block, preferred_element_type=F32
        )
    return (jnp.concatenate(query_grads, axis=1), key_grad, value_grad)


def build(F, C):
    Z = C // 2

    def per_device(
        hidden_in,
        segment_ids,
        positions,
        norm1_gain,
        norm1_bias,
        query_weight,
        query_bias,
        keyval_weight,
        value_bias,
        out_weight,
        out_bias,
        norm2_gain,
        norm2_bias,
        fc_weight,
        fc_bias,
        proj_weight,
        proj_bias,
        out_grad,
    ):
        micros, rows = hidden_in.shape[:2]
        tok = micros * rows
        scale = 1.0 / math.sqrt(HD)
        head_block = 1
        while head_block * rows < 512 and head_block < HEADS:
            head_block = head_block * 2
        f = lax.axis_index("fsdp")
        k = lax.axis_index("ctx")
        core = k % 2
        quad = k % QUAD
        zi = k // 2
        hsh = D // F
        width = fc_weight.shape[1] // F // QUAD

        def pick_core(a, b):
            return jnp.where(core == 0, a, b)

        def in_order(own, other):
            return pick_core(
                jnp.concatenate([own, other], axis=1), jnp.concatenate([other, own], axis=1)
            )

        def halves(x):
            w = x.shape[1] // 2
            return pick_core(x[:, :w], x[:, w:]), pick_core(x[:, w:], x[:, :w])

        def after(x, *deps):
            return lax.optimization_barrier((x,) + deps)[0]

        def swk(x, bit):
            return swap_k(x, bit, C)

        def gather_ctx(x):
            held = {0: x}
            for bit in bits_of(C)[1:][::-1] + [1]:
                for d in list(held):
                    held[d ^ bit] = swk(held[d], bit)
            return [held[d] for d in range(C)]

        def gather_quad(x):
            a = swk(x, 1)
            b = swk(x, 2)
            c = swk(b, 1)
            return [x, a, b, c]

        names = (
            norm1_gain, norm1_bias, query_bias, out_bias, norm2_gain, norm2_bias, proj_bias,
            fc_bias, value_bias,
        )
        sizes = [v.shape[0] for v in names]
        packed = jnp.concatenate(names)
        pad = -packed.shape[0] % 1024
        packed = jnp.pad(packed, (0, pad)).reshape(-1, 128)
        vec = jnp.zeros((F,) + packed.shape, BF16)
        for d in range(F):
            part = packed if d == 0 else swap_f(packed, d, F)
            vec = lax.dynamic_update_slice(vec, part[None], (f ^ d, 0, 0))
        vec = vec.reshape(F, -1).astype(F32)
        full = []
        at = 0
        for size in sizes:
            full.append(vec[:, at : at + size])
            at += size
        gain_one, shift_one, b_query, b_out, gain_two, shift_two, b_proj = [
            v.reshape(-1) for v in full[:7]
        ]
        b_value = full[8].reshape(-1)
        b_fc = lax.dynamic_slice(
            full[7].reshape(F, QUAD, width), (0, quad, 0), (F, 1, width)
        ).reshape(-1)
        kv_bias = jnp.concatenate([jnp.zeros((HD,), F32), b_value])

        places = jnp.concatenate([segment_ids, positions], axis=0)
        places = jnp.stack(gather_ctx(places), axis=1)
        seg_all = places[:micros].reshape(micros, -1)
        pos_all = places[micros:].reshape(micros, -1)

        w_keyval = gather_f(keyval_weight, f, F)
        wq_piece = halves(query_weight)[0]
        wq_own = gather_f(after(wq_piece, w_keyval), f, F)
        wq_other = swk(wq_own, 1)
        wo_piece = halves(out_weight)[0]
        wo_own = gather_f(after(wo_piece, wq_own), f, F)
        wo_other = swk(wo_own, 1)

        fc_view = fc_weight.reshape(hsh, F, QUAD, width)
        fc_piece = fc_view[:, :, 0]
        for i in range(1, QUAD):
            fc_piece = jnp.where(quad == i, fc_view[:, :, i], fc_piece)
        fc_piece = fc_piece.reshape(hsh, F * width)
        proj_piece = lax.dynamic_slice(proj_weight, (quad * width, 0), (width, D))
        w_fc = gather_f(after(fc_piece, wo_own), f, F)
        w_proj = gather_f(after(proj_piece, w_fc), f, F)

        hidden = hidden_in.reshape(tok, D).astype(F32)
        normed1 = layer_norm(hidden, gain_one, shift_one).astype(BF16)
        keyvals = (dot(normed1, w_keyval) + kv_bias).astype(BF16)
        group_kv = jnp.stack(gather_ctx(keyvals.reshape(micros, rows, 2 * HD)), axis=1)
        group_kv = group_kv.reshape(micros, C * rows, 2 * HD)
        queries = (in_order(dot(normed1, wq_own), dot(normed1, wq_other)) + b_query).astype(BF16)
        queries = queries.reshape(micros, rows, HEADS, HD)
        visible = [
            (pos_all[m][None, :] <= positions[m][:, None])
            & ((seg_all[m][None, :] == 0) | (seg_all[m][None, :] == segment_ids[m][:, None]))
            for m in range(micros)
        ]
        mixed = []
        lse = []
        middle = []
        normed2_blocks = []
        for m in range(micros):
            out, lse_rows = attend_forward(
                queries[m], group_kv[m, :, :HD], group_kv[m, :, HD:], visible[m], head_block, scale
            )
            mix = out.reshape(rows, D).astype(BF16)
            mixed.append(mix)
            lse.append(lse_rows)
            mid = (
                hidden[m * rows : (m + 1) * rows]
                + in_order(dot(mix, wo_own), dot(mix, wo_other))
                + b_out
            )
            middle.append(mid)
            normed2_blocks.append(gather_quad(layer_norm(mid, gain_two, shift_two).astype(BF16)))
        mixed = jnp.concatenate(mixed, axis=0)
        middle = jnp.concatenate(middle, axis=0)
        normed2 = jnp.concatenate(
            [normed2_blocks[m][d] for d in range(QUAD) for m in range(micros)], axis=0
        )
        cot_own = out_grad.reshape(tok, D)
        cot = jnp.concatenate(gather_quad(cot_own), axis=0)

        active, slope = gelu_and_slope(dot(normed2, w_fc) + b_fc)
        active = active.astype(BF16)
        slope = slope.astype(BF16)

        def cols(x, d):
            w = x.shape[1] // F
            return lax.dynamic_slice(x, (0, (f ^ d) * w), (x.shape[0], w))

        def weight_grad(left, right):
            w = right.shape[1] // 2
            return reduce_f(lambda d, h: t_dot(cols(left, d), right[:, h * w : (h + 1) * w]), F)

        proj_grad = weight_grad(active, cot)

        def reduce_quad(term):
            outs = []
            for m in range(micros):
                r2 = swk(term(3, m).astype(BF16), 1)
                r0 = swk(term(1, m).astype(BF16), 1)
                z0 = swk((term(2, m) + r2.astype(F32)).astype(BF16), 2)
                outs.append(term(0, m) + r0.astype(F32) + z0.astype(F32))
            return outs

        def block(x, d, m):
            at = d * tok + m * rows
            return x[at : at + rows]

        d_before = (dot_t(cot, w_proj) * slope.astype(F32)).astype(BF16)
        d_normed2 = reduce_quad(lambda d, m: dot_t(block(d_before, d, m), w_fc))
        fc_grad = weight_grad(normed2, d_before)
        fc_b_grad = jnp.sum(d_before.astype(F32), axis=0)
        ffn = reduce_quad(lambda d, m: dot(block(active, d, m), w_proj))
        result = middle + jnp.concatenate(ffn, axis=0) + b_proj
        hidden_out = result.astype(BF16).reshape(micros, rows, D)

        d_middle, gain_two_grad, shift_two_grad = layer_norm_back(
            middle, gain_two, jnp.concatenate(d_normed2, axis=0)
        )
        d_middle = cot_own.astype(F32) + d_middle
        d_branch = d_middle.astype(BF16)
        branch_own, branch_other = halves(d_branch)
        d_mixed = (dot_t(branch_own, wo_own) + dot_t(branch_other, wo_other)).astype(BF16)
        branch_pair = jnp.concatenate([branch_own, swk(branch_other, 1)], axis=0)
        mixed_pair = jnp.concatenate([mixed, swk(mixed, 1)], axis=0)
        normed1_pair = jnp.concatenate([normed1, swk(normed1, 1)], axis=0)
        out_w_grad = weight_grad(mixed_pair, branch_pair)
        d_mixed = d_mixed.reshape(micros, rows, HEADS, HD)
        d_queries = []
        d_keyvals = []
        for m in range(micros):
            grad_queries, key_grad, value_grad = attend_backward(
                queries[m],
                group_kv[m, :, :HD],
                group_kv[m, :, HD:],
                visible[m],
                lse[m],
                d_mixed[m],
                head_block,
                scale,
            )
            d_queries.append(grad_queries.reshape(rows, D).astype(BF16))
            terms = jnp.concatenate([key_grad, value_grad], axis=1).reshape(C, rows, 2 * HD)
            terms = {d: terms[d] for d in range(C)}
            for bit in [1] + bits_of(C)[1:][::-1]:
                sent = [d for d in terms if d & bit]
                got = swk(jnp.stack([terms[d] for d in sent]).astype(BF16), bit)
                for i, d in enumerate(sent):
                    terms[d ^ bit] = terms[d ^ bit] + got[i].astype(F32)
                    del terms[d]
            d_keyvals.append(terms[0].astype(BF16))
        d_queries = jnp.concatenate(d_queries, axis=0)
        d_keyvals = jnp.concatenate(d_keyvals, axis=0)
        dq_own, dq_other = halves(d_queries)
        dq_pair = jnp.concatenate([dq_own, swk(dq_other, 1)], axis=0)
        query_w_grad = weight_grad(normed1_pair, dq_pair)
        keyval_w_grad = weight_grad(normed1, d_keyvals)
        d_normed1 = (
            dot_t(dq_own, wq_own) + dot_t(dq_other, wq_other) + dot_t(d_keyvals, w_keyval)
        )
        d_hidden, gain_one_grad, shift_one_grad = layer_norm_back(hidden, gain_one, d_normed1)
        hidden_grad = (d_middle + d_hidden).reshape(micros, rows, D)

        def sum_z(x):
            part = x.shape[0] // Z
            blocks = x.astype(BF16).reshape(Z, part, x.shape[1])

            def one(d):
                return lax.dynamic_slice(blocks, (zi ^ d, 0, 0), (1,) + blocks.shape[1:])[0]

            total = one(0).astype(F32)
            for d in range(1, Z):
                total = total + swk(one(d), 2 * d).astype(F32)
            total = total.astype(BF16)
            out = jnp.zeros(blocks.shape, BF16)
            for d in range(Z):
                got = total if d == 0 else swk(total, 2 * d)
                out = lax.dynamic_update_slice(out, got[None], (zi ^ d, 0, 0))
            own = out.reshape(x.shape)
            return in_order(own, swk(own, 1)).astype(F32)

        def sum_quads(x):
            for bit in bits_of(C)[2:]:
                x = x + swk(x.astype(BF16), bit).astype(F32)
            parts = gather_quad(x.astype(BF16))
            out = jnp.zeros((QUAD,) + x.shape, BF16)
            for d in range(QUAD):
                out = lax.dynamic_update_slice(out, parts[d][None], (quad ^ d, 0, 0))
            return out

        proj_out = sum_quads(proj_grad).reshape(QUAD * width, D).astype(F32)
        fc_parts = sum_quads(fc_grad)
        fc_out = jnp.concatenate(
            [
                fc_parts[i][:, j * width : (j + 1) * width]
                for j in range(F)
                for i in range(QUAD)
            ],
            axis=1,
        ).astype(F32)
        out_out = sum_z(out_w_grad)
        query_out = sum_z(query_w_grad)
        kv_sum = keyval_w_grad
        for bit in bits_of(C):
            kv_sum = kv_sum + swk(kv_sum.astype(BF16), bit).astype(F32)

        fc_b_full = lax.dynamic_update_slice(
            jnp.zeros((F, QUAD, width), F32), fc_b_grad.reshape(F, 1, width), (0, quad, 0)
        )

        def sum_vectors(vectors):
            sizes = [v.size // F for v in vectors]
            packed = jnp.concatenate([v.reshape(F, -1) for v in vectors], axis=1)
            packed = jnp.pad(packed, ((0, 0), (0, -packed.shape[1] % 1024)))
            packed = packed.reshape(F, -1, 128)

            def one(d):
                return lax.dynamic_slice(packed, (f ^ d, 0, 0), (1,) + packed.shape[1:])[0]

            total = one(0)
            for d in range(1, F):
                total = total + swap_f(one(d), d, F)
            for bit in bits_of(C):
                total = total + swk(total, bit)
            total = total.reshape(-1)
            outs = []
            at = 0
            for size in sizes:
                outs.append(total[at : at + size])
                at += size
            return outs

        def column_sum(x):
            return jnp.sum(x.astype(F32), axis=0)

        g2, s2, bp, bo, bf = sum_vectors(
            [gain_two_grad, shift_two_grad, column_sum(cot_own), column_sum(d_branch), fc_b_full]
        )
        g1, s1, bq, bv = sum_vectors(
            [
                gain_one_grad,
                shift_one_grad,
                column_sum(d_queries),
                column_sum(d_keyvals[:, HD:]),
            ]
        )
        return (
            hidden_out, hidden_grad, g1, s1, query_out, bq, kv_sum, bv, out_out, bo, g2, s2,
            fc_out, bf, proj_out, bp,
        )

    return per_device


def solution(mesh):
    tokens = P(None, ("fsdp", "ctx"), None)
    places = P(None, ("fsdp", "ctx"))
    vec = P("fsdp")
    mat = P("fsdp", None)
    grads = (vec, vec, mat, vec, mat, vec, mat, vec, vec, vec, mat, vec, mat, vec)
    return jax.shard_map(
        build(mesh.shape["fsdp"], mesh.shape["ctx"]),
        mesh=mesh,
        in_specs=(tokens, places, places) + grads + (tokens,),
        out_specs=(tokens, tokens) + grads,
        check_vma=False,
    )
```

```python
import functools
import math

import jax
import jax.numpy as jnp
from jax import lax
from jax.experimental import pallas as pl
from jax.experimental.pallas import tpu as pltpu
from jax.sharding import PartitionSpec as P

D = 2048
HEADS = 16
HD = 128
QUAD = 4
F32 = jnp.float32
BF16 = jnp.bfloat16


def layer_norm(values, gain, shift):
    center = jnp.mean(values, axis=-1, keepdims=True)
    shifted = values - center
    spread = jnp.mean(shifted * shifted, axis=-1, keepdims=True)
    return shifted * lax.rsqrt(spread + 1e-05) * gain + shift


def layer_norm_back(values, gain, d_out):
    center = jnp.mean(values, axis=-1, keepdims=True)
    shifted = values - center
    spread = jnp.mean(shifted * shifted, axis=-1, keepdims=True)
    r = lax.rsqrt(spread + 1e-05)
    xhat = shifted * r
    e = d_out * gain
    d_values = r * (
        e - jnp.mean(e, axis=-1, keepdims=True) - xhat * jnp.mean(e * xhat, axis=-1, keepdims=True)
    )
    return d_values, jnp.sum(d_out * xhat, axis=0), jnp.sum(d_out, axis=0)


def gelu_and_slope(u):
    a = math.sqrt(2.0 / math.pi)
    t = jnp.tanh(a * (u + 0.044715 * u * u * u))
    half = 0.5 * (1.0 + t)
    slope = half + 0.5 * u * (1.0 - t * t) * a * (1.0 + 3.0 * 0.044715 * u * u)
    return u * half, slope


def dot(a, b):
    return jnp.dot(a, b, preferred_element_type=F32)


def dot_t(a, b):
    return lax.dot_general(a, b, (((1,), (1,)), ((), ())), preferred_element_type=F32)


def t_dot(a, b):
    return lax.dot_general(a, b, (((0,), (0,)), ((), ())), preferred_element_type=F32)


def swap_f(x, bit, size):
    return lax.ppermute(x, "fsdp", [(i, i ^ bit) for i in range(size)])


def swap_k(x, bit, size):
    return lax.ppermute(x, "ctx", [(i, i ^ bit) for i in range(size)])


def bits_of(size):
    out = []
    bit = 1
    while bit < size:
        out.append(bit)
        bit *= 2
    return out


def flip(index, d):
    bit = 1
    while bit <= d:
        if d & bit:
            index = index + bit * (1 - 2 * ((index // bit) % 2))
        bit *= 2
    return index


def head_kernel(
    F, C, vec_ref, place_ref, wkv_ref, wq_ref, vec_out, place_out, wkv_out, wq_out, send, recv, local
):
    f = lax.axis_index("fsdp")
    k = lax.axis_index("ctx")
    core = k % 2
    barrier = pltpu.get_barrier_semaphore()
    partners = [{"fsdp": flip(f, bit)} for bit in bits_of(F)]
    partners += [{"ctx": flip(k, bit)} for bit in bits_of(C)]
    for partner in partners:
        pl.semaphore_signal(barrier, inc=1, device_id=partner, device_id_type=pl.DeviceIdType.MESH)
    pl.semaphore_wait(barrier, len(partners))

    count = [0]
    started = []

    def remote(src, dst, partner):
        n = count[0]
        count[0] += 1
        copy = pltpu.make_async_remote_copy(
            src_ref=src,
            dst_ref=dst,
            send_sem=send.at[n],
            recv_sem=recv.at[n],
            device_id=partner,
            device_id_type=pl.DeviceIdType.MESH,
        )
        copy.start()
        started.append(copy)
        return copy

    own_copies = []

    def keep(src, dst):
        copy = pltpu.make_async_copy(src, dst, local.at[len(own_copies)])
        copy.start()
        own_copies.append(copy)

    def tree(own, place, order, me, axis, handed=None):
        come = {}

        def sends(d, position):
            for p in range(position, len(order)):
                src = own if d == 0 else place(d, d)
                copy = remote(src, place(d ^ order[p], d), {axis: flip(me, order[p])})
                come[d ^ order[p]] = (copy, p + 1)

        sends(0, 0)
        yield
        done = {0}
        while len(done) < len(come) + 1:
            for d in list(come):
                if d in done:
                    continue
                copy, position = come[d]
                copy.wait_recv()
                done.add(d)
                sends(d, position)
                if handed is not None:
                    handed(place(d, d))
                yield

    vec_rows = vec_ref.shape[0]
    trees = [
        tree(vec_ref, lambda d, e: vec_out.at[flip(f, e)], bits_of(F), f, "fsdp"),
    ]
    keep(vec_ref, vec_out.at[f])
    arrivals = []
    for ref, out in ((wkv_ref, wkv_out), (wq_ref, wq_out)):
        rows, width = ref.shape
        half, wide = rows // 2, width // 2
        columns = pl.ds(pl.multiple_of(core * wide, wide), wide)
        keep(ref, out.at[pl.ds(pl.multiple_of(f * rows, rows), rows)])
        for h, order in enumerate((bits_of(F), bits_of(F)[::-1])):

            def place(d, e, out=out, h=h, rows=rows, half=half, columns=columns):
                start = flip(f, e) * rows + h * half
                return out.at[pl.ds(pl.multiple_of(start, half), half), columns]

            def handed(block):
                arrivals.append(remote(block, block, {"ctx": flip(k, 1)}))

            own = ref.at[pl.ds(h * half, half), columns]
            trees.append(tree(own, place, order, f, "fsdp", handed))
    keep(place_ref, place_out.at[0])
    trees.append(tree(place_ref, lambda d, e: place_out.at[d], bits_of(C)[::-1], k, "ctx"))
    while trees:
        for one in list(trees):
            try:
                next(one)
            except StopIteration:
                trees.remove(one)
    for copy in arrivals:
        copy.wait_recv()
    for copy in started:
        copy.wait_send()
    for copy in own_copies:
        copy.wait()


def gather_head(F, C, vec, place, wkv, wq):
    copies = (F - 1) + (C - 1) + 2 * 2 * 2 * (F - 1)
    return pl.pallas_call(
        functools.partial(head_kernel, F, C),
        in_specs=[pl.BlockSpec(memory_space=pl.ANY)] * 4,
        out_specs=[pl.BlockSpec(memory_space=pl.ANY)] * 4,
        out_shape=[
            jax.ShapeDtypeStruct((F,) + vec.shape, vec.dtype),
            jax.ShapeDtypeStruct((C,) + place.shape, place.dtype),
            jax.ShapeDtypeStruct((F * wkv.shape[0], wkv.shape[1]), wkv.dtype),
            jax.ShapeDtypeStruct((F * wq.shape[0], wq.shape[1]), wq.dtype),
        ],
        scratch_shapes=[
            pltpu.SemaphoreType.DMA((copies,)),
            pltpu.SemaphoreType.DMA((copies,)),
            pltpu.SemaphoreType.DMA((4,)),
        ],
        compiler_params=pltpu.CompilerParams(collective_id=0, has_side_effects=True),
        name="gather_head",
    )(vec, place, wkv, wq)


HEAD_STEP = 2
KEY_STEP = 512


def forward_kernel(scale, q_ref, kv_ref, kplace_ref, qplace_ref, o_ref, lse_ref, bias, vt_ref, sc):
    keys = kv_ref.shape[0]

    @pl.when(pl.program_id(0) == 0)
    def _():
        fill_bias(kplace_ref, qplace_ref, bias)
        for at in range(0, keys, KEY_STEP):
            vt_ref[:, at : at + KEY_STEP] = kv_ref[at : at + KEY_STEP, HD:].T

    for h in range(HEAD_STEP):
        q = q_ref[:, h * HD : (h + 1) * HD]
        peak = None
        for at in range(0, keys, KEY_STEP):
            s = dot_t(kv_ref[at : at + KEY_STEP, :HD], q) * scale + bias[at : at + KEY_STEP]
            sc[h, at : at + KEY_STEP] = s
            top = jnp.max(s, axis=0, keepdims=True)
            peak = top if peak is None else jnp.maximum(peak, top)
        total = jnp.zeros_like(peak)
        acc = jnp.zeros((HD, q.shape[0]), F32)
        for at in range(0, keys, KEY_STEP):
            p = jnp.exp(sc[h, at : at + KEY_STEP] - peak)
            total = total + jnp.sum(p, axis=0, keepdims=True)
            acc = acc + dot(vt_ref[:, at : at + KEY_STEP], p.astype(BF16))
        o_ref[:, h * HD : (h + 1) * HD] = (acc / total).T.astype(BF16)
        lse_ref[0, h : h + 1] = peak + jnp.log(total)


def fill_bias(kplace_ref, qplace_ref, bias):
    for at in range(0, bias.shape[0], KEY_STEP):
        seg_k = kplace_ref[at : at + KEY_STEP, 0:1]
        pos_k = kplace_ref[at : at + KEY_STEP, 1:2]
        seg_q = qplace_ref[0:1]
        pos_q = qplace_ref[1:2]
        seen = (pos_k <= pos_q) & ((seg_k == 0) | (seg_k == seg_q))
        bias[at : at + KEY_STEP] = jnp.where(seen, 0.0, -1e30)


def backward_kernel(
    scale, q_ref, do_ref, o_ref, lse_ref, kv_ref, kplace_ref, qplace_ref, dq_ref, dkv_ref, bias, kt_ref
):
    keys = kv_ref.shape[0]

    @pl.when(pl.program_id(0) == 0)
    def _():
        fill_bias(kplace_ref, qplace_ref, bias)
        dkv_ref[...] = jnp.zeros_like(dkv_ref)
        for at in range(0, keys, KEY_STEP):
            kt_ref[:, at : at + KEY_STEP] = kv_ref[at : at + KEY_STEP, :HD].T

    for h in range(HEAD_STEP):
        q = q_ref[:, h * HD : (h + 1) * HD]
        do = do_ref[:, h * HD : (h + 1) * HD]
        o = o_ref[:, h * HD : (h + 1) * HD]
        inner = jnp.sum((do.astype(F32) * o.astype(F32)).T, axis=0, keepdims=True)
        lse = lse_ref[0, h : h + 1]
        dq = jnp.zeros((HD, q.shape[0]), F32)
        for at in range(0, keys, KEY_STEP):
            rows = slice(at, at + KEY_STEP)
            s = dot_t(kv_ref[rows, :HD], q) * scale + bias[rows]
            p = jnp.exp(s - lse)
            dp = dot_t(kv_ref[rows, HD:], do)
            ds = (p * (dp - inner)).astype(BF16)
            dkv_ref[rows, HD:] += dot(p.astype(BF16), do)
            dkv_ref[rows, :HD] += dot(ds, q)
            dq = dq + dot(kt_ref[:, rows], ds)
        dq_ref[:, h * HD : (h + 1) * HD] = (dq * scale).T.astype(BF16)


def attend_forward(queries, kv, kplace, qplace, scale):
    rows = queries.shape[0]
    keys = kv.shape[0]
    whole = lambda x: pl.BlockSpec(x.shape, lambda h: (0,) * x.ndim)
    heads = pl.BlockSpec((rows, HEAD_STEP * HD), lambda h: (0, h))
    return pl.pallas_call(
        functools.partial(forward_kernel, scale),
        grid=(HEADS // HEAD_STEP,),
        in_specs=[heads, whole(kv), whole(kplace), whole(qplace)],
        out_specs=[heads, pl.BlockSpec((1, HEAD_STEP, rows), lambda h: (h, 0, 0))],
        out_shape=[
            jax.ShapeDtypeStruct((rows, HEADS * HD), BF16),
            jax.ShapeDtypeStruct((HEADS // HEAD_STEP, HEAD_STEP, rows), F32),
        ],
        scratch_shapes=[
            pltpu.VMEM((keys, rows), F32),
            pltpu.VMEM((HD, keys), BF16),
            pltpu.VMEM((HEAD_STEP, keys, rows), F32),
        ],
        compiler_params=pltpu.CompilerParams(vmem_limit_bytes=32 * 1024 * 1024),
        cost_estimate=pl.CostEstimate(
            flops=8 * rows * keys * HEADS * HD,
            bytes_accessed=4 * rows * HEADS * HD,
            transcendentals=rows * keys * HEADS,
        ),
        name="attend_forward",
    )(queries, kv, kplace, qplace)


def attend_backward(queries, d_mixed, mixed, lse, kv, kplace, qplace, scale):
    rows = queries.shape[0]
    keys = kv.shape[0]
    whole = lambda x: pl.BlockSpec(x.shape, lambda h: (0,) * x.ndim)
    heads = pl.BlockSpec((rows, HEAD_STEP * HD), lambda h: (0, h))
    return pl.pallas_call(
        functools.partial(backward_kernel, scale),
        grid=(HEADS // HEAD_STEP,),
        in_specs=[
            heads,
            heads,
            heads,
            pl.BlockSpec((1, HEAD_STEP, rows), lambda h: (h, 0, 0)),
            whole(kv),
            whole(kplace),
            whole(qplace),
        ],
        out_specs=[heads, pl.BlockSpec((keys, 2 * HD), lambda h: (0, 0))],
        out_shape=[
            jax.ShapeDtypeStruct((rows, HEADS * HD), BF16),
            jax.ShapeDtypeStruct((keys, 2 * HD), F32),
        ],
        scratch_shapes=[pltpu.VMEM((keys, rows), F32), pltpu.VMEM((HD, keys), BF16)],
        compiler_params=pltpu.CompilerParams(vmem_limit_bytes=32 * 1024 * 1024),
        cost_estimate=pl.CostEstimate(
            flops=18 * rows * keys * HEADS * HD,
            bytes_accessed=8 * rows * HEADS * HD,
            transcendentals=rows * keys * HEADS,
        ),
        name="attend_backward",
    )(queries, d_mixed, mixed, lse, kv, kplace, qplace)


def build(F, C):
    Z = C // 2

    def per_device(
        hidden_in,
        segment_ids,
        positions,
        norm1_gain,
        norm1_bias,
        query_weight,
        query_bias,
        keyval_weight,
        value_bias,
        out_weight,
        out_bias,
        norm2_gain,
        norm2_bias,
        fc_weight,
        fc_bias,
        proj_weight,
        proj_bias,
        out_grad,
    ):
        micros, rows = hidden_in.shape[:2]
        tok = micros * rows
        scale = 1.0 / math.sqrt(HD)
        f = lax.axis_index("fsdp")
        k = lax.axis_index("ctx")
        core = k % 2
        quad = k % QUAD
        zi = k // 2
        hsh = D // F
        width = fc_weight.shape[1] // F // QUAD

        def pick_core(a, b):
            return jnp.where(core == 0, a, b)

        def in_order(own, other):
            return pick_core(
                jnp.concatenate([own, other], axis=1), jnp.concatenate([other, own], axis=1)
            )

        def halves(x):
            w = x.shape[1] // 2
            return pick_core(x[:, :w], x[:, w:]), pick_core(x[:, w:], x[:, :w])

        def after(x, *deps):
            return lax.optimization_barrier((x,) + deps)[0]

        def behind(x, *deps):
            zero = sum(
                jnp.minimum(jnp.abs(d[(slice(0, 1),) * d.ndim].reshape(()).astype(F32)), 0.0)
                for d in deps
            )
            return (x.astype(F32) + zero).astype(x.dtype)

        def swk(x, bit):
            return swap_k(x, bit, C)

        def gather_ctx(x):
            held = {0: x}
            for bit in bits_of(C)[1:][::-1] + [1]:
                for d in list(held):
                    held[d ^ bit] = swk(held[d], bit)
            return [held[d] for d in range(C)]

        def gather_quad(x):
            a = swk(x, 1)
            b = swk(x, 2)
            c = swk(b, 1)
            return [x, b, a, c]

        names = (
            norm1_gain, norm1_bias, query_bias, out_bias, norm2_gain, norm2_bias, proj_bias,
            fc_bias, value_bias,
        )
        sizes = [v.shape[0] for v in names]
        packed = jnp.concatenate(names)
        pad = -packed.shape[0] % 2048
        packed = jnp.pad(packed, (0, pad)).reshape(-1, 128)
        places = jnp.concatenate([segment_ids, positions], axis=0)
        vec, places, w_keyval, w_query = gather_head(
            F, C, packed, places, keyval_weight, query_weight
        )
        vec = vec.reshape(F, -1).astype(F32)
        full = []
        at = 0
        for size in sizes:
            full.append(vec[:, at : at + size])
            at += size
        gain_one, shift_one, b_query, b_out, gain_two, shift_two, b_proj = [
            v.reshape(-1) for v in full[:7]
        ]
        b_value = full[8].reshape(-1)
        b_fc = lax.dynamic_slice(
            full[7].reshape(F, QUAD, width), (0, quad, 0), (F, 1, width)
        ).reshape(-1)
        kv_bias = jnp.concatenate([jnp.zeros((HD,), F32), b_value])

        seg_all = [places[:, m].reshape(-1) for m in range(micros)]
        pos_all = [places[:, micros + m].reshape(-1) for m in range(micros)]

        wo_own = lax.all_gather(halves(out_weight)[0], "fsdp", axis=0, tiled=True)
        wo_other = swk(wo_own, 1)

        fc_piece = jnp.concatenate(
            [
                lax.dynamic_slice(fc_weight, (0, (j * QUAD + quad) * width), (hsh, width))
                for j in range(F)
            ],
            axis=1,
        )
        proj_piece = lax.dynamic_slice(proj_weight, (quad * width, 0), (width, D))
        w_fc = lax.all_gather(fc_piece, "fsdp", axis=0, tiled=True)
        w_proj = lax.all_gather(proj_piece, "fsdp", axis=0, tiled=True)

        hidden = hidden_in.reshape(tok, D).astype(F32)
        normed1 = layer_norm(hidden, gain_one, shift_one).astype(BF16)
        keyvals = (dot(normed1, w_keyval) + kv_bias).astype(BF16)
        group_kv = jnp.concatenate(
            gather_ctx(keyvals.reshape(micros, rows, 2 * HD)), axis=1
        )
        queries = (dot(normed1, w_query) + b_query).astype(BF16)
        kplace = [jnp.stack([seg_all[m], pos_all[m]], axis=1) for m in range(micros)]
        qplace = [jnp.stack([segment_ids[m], positions[m]]) for m in range(micros)]
        queries = [queries[m * rows : (m + 1) * rows] for m in range(micros)]
        mixed = []
        lse = []
        middle = []
        normed2_blocks = []
        for m in range(micros):
            mix, lse_rows = attend_forward(
                queries[m], group_kv[m], kplace[m], qplace[m], scale
            )
            mixed.append(mix)
            lse.append(lse_rows)
            mid = (
                hidden[m * rows : (m + 1) * rows]
                + in_order(dot(mix, wo_own), dot(mix, wo_other))
                + b_out
            )
            middle.append(mid)
            normed2_blocks.append(gather_quad(layer_norm(mid, gain_two, shift_two).astype(BF16)))
        all_mixed = jnp.concatenate(mixed, axis=0)
        middle = jnp.concatenate(middle, axis=0)
        normed2 = jnp.concatenate(
            [normed2_blocks[m][d] for d in range(QUAD) for m in range(micros)], axis=0
        )
        cot_own = out_grad.reshape(tok, D)
        cot = jnp.concatenate(gather_quad(after(cot_own, group_kv)), axis=0)

        active, slope = gelu_and_slope(dot(normed2, w_fc) + b_fc)
        active = active.astype(BF16)
        slope = slope.astype(BF16)

        def scatter(term):
            return lax.psum_scatter(term, "fsdp", scatter_dimension=0, tiled=True)

        def ffn_grad(left, right):
            term = t_dot(left, right).astype(BF16)
            return lax.psum_scatter(term, "fsdp", scatter_dimension=0, tiled=True), term

        proj_grad, proj_term = ffn_grad(active, cot)

        def reduce_quad(x, product):
            got = swk(product(x[2 * tok :]).astype(BF16), 1).astype(F32)
            passed = (product(x[tok : 2 * tok]) + got[tok:]).astype(BF16)
            own = product(x[:tok]) + got[:tok]
            outs = []
            for m in range(micros):
                at = slice(m * rows, (m + 1) * rows)
                outs.append(own[at] + swk(passed[at], 2).astype(F32))
            return outs

        d_before = (dot_t(after(cot, proj_term), w_proj) * slope.astype(F32)).astype(BF16)
        d_normed2 = reduce_quad(d_before, lambda x: dot_t(x, w_fc))
        fc_grad, fc_term = ffn_grad(normed2, d_before)
        fc_b_grad = jnp.sum(d_before.astype(F32), axis=0)

        d_middle, gain_two_grad, shift_two_grad = layer_norm_back(
            middle, gain_two, jnp.concatenate(d_normed2, axis=0)
        )
        d_middle = cot_own.astype(F32) + d_middle
        d_branch = d_middle.astype(BF16)
        branch_own, branch_other = halves(d_branch)
        d_mixed = (dot_t(branch_own, wo_own) + dot_t(branch_other, wo_other)).astype(BF16)
        def across_quads(x):
            for bit in bits_of(C)[2:]:
                cut = x.shape[0] // 2
                first = swk(x[:cut], bit)
                second = swk(behind(x[cut:], first), bit)
                got = jnp.concatenate([first, second])
                x = (x.astype(F32) + got.astype(F32)).astype(BF16)
            return x

        d_mixed = behind(d_mixed, proj_grad)
        proj_sum = across_quads(proj_grad)
        d_mixed = [d_mixed[m * rows : (m + 1) * rows] for m in range(micros)]
        kv_scale = jnp.concatenate([jnp.full((HD,), scale, F32), jnp.ones((HD,), F32)])
        d_queries = []
        d_keyvals = []
        for m in range(micros):
            dq, dkv = attend_backward(
                queries[m], d_mixed[m], mixed[m], lse[m], group_kv[m], kplace[m], qplace[m], scale
            )
            d_queries.append(dq)
            terms = (dkv * kv_scale).reshape(C, rows, 2 * HD)
            terms = {d: terms[d] for d in range(C)}
            for bit in [1] + bits_of(C)[1:][::-1]:
                sent = [d for d in terms if d & bit]
                got = swk(jnp.stack([terms[d] for d in sent]).astype(BF16), bit)
                for i, d in enumerate(sent):
                    terms[d ^ bit] = terms[d ^ bit] + got[i].astype(F32)
                    del terms[d]
            d_keyvals.append(terms[0].astype(BF16))
        d_queries = jnp.concatenate(d_queries, axis=0)
        d_keyvals = jnp.concatenate(d_keyvals, axis=0)
        fc_sum = across_quads(fc_grad)
        dq_own, dq_other = halves(d_queries)
        dq_pair = jnp.concatenate([dq_own, swk(dq_other, 1)], axis=0)
        normed1_pair = jnp.concatenate([normed1, swk(normed1, 1)], axis=0)
        query_term = t_dot(normed1_pair, dq_pair).astype(BF16)
        query_w_grad = scatter(query_term)
        branch_own, branch_other = halves(behind(d_branch, query_term))
        branch_pair = jnp.concatenate([branch_own, swk(branch_other, 1)], axis=0)
        mixed_pair = jnp.concatenate([all_mixed, swk(all_mixed, 1)], axis=0)
        out_term = t_dot(mixed_pair, branch_pair).astype(BF16)
        out_w_grad = scatter(out_term)
        ffn = reduce_quad(after(active, fc_term), lambda x: dot(x, w_proj))
        result = middle + jnp.concatenate(ffn, axis=0) + b_proj
        hidden_out = result.astype(BF16).reshape(micros, rows, D)
        keyval_w_grad = scatter(t_dot(normed1, d_keyvals).astype(BF16)).astype(F32)
        d_normed1 = (
            dot_t(d_queries, w_query) + dot_t(behind(d_keyvals, proj_sum), w_keyval)
        )
        d_hidden, gain_one_grad, shift_one_grad = layer_norm_back(hidden, gain_one, d_normed1)
        hidden_grad = (d_middle + d_hidden).reshape(micros, rows, D)

        def sum_z(x):
            part = x.shape[0] // Z
            blocks = x.astype(BF16).reshape(Z, part, x.shape[1])
            terms = [
                lax.dynamic_slice(blocks, (zi ^ d, 0, 0), (1,) + blocks.shape[1:])[0].astype(F32)
                for d in range(Z)
            ]
            terms = dict(enumerate(terms))
            for bit in bits_of(Z):
                sent = [d for d in terms if d & bit]
                got = swk(jnp.concatenate([terms[d] for d in sent]).astype(BF16), 2 * bit)
                for i, d in enumerate(sent):
                    terms[d ^ bit] = terms[d ^ bit] + got[i * part : (i + 1) * part].astype(F32)
                    del terms[d]
            held = terms[0].astype(BF16)
            ids = [0]
            for bit in bits_of(Z)[::-1]:
                held = jnp.concatenate([held, swk(held, 2 * bit)])
                ids = ids + [d ^ bit for d in ids]
            out = jnp.full(blocks.shape, 0.125, BF16)
            for i, d in enumerate(ids):
                block = held[i * part : (i + 1) * part]
                out = lax.dynamic_update_slice(out, block[None], (zi ^ d, 0, 0))
            own = out.reshape(x.shape)
            return in_order(own, swk(own, 1)).astype(F32)

        members = (0, 2, 1, 3)
        proj_out = jnp.full((QUAD * width, D), 1.0, F32)
        for d, part in zip(members, gather_quad(proj_sum)):
            proj_out = lax.dynamic_update_slice(proj_out, part.astype(F32), ((quad ^ d) * width, 0))
        fc_parts = jnp.full((QUAD, hsh, F * width), 0.75, BF16)
        for d, part in zip(members, gather_quad(fc_sum)):
            fc_parts = lax.dynamic_update_slice(fc_parts, part[None], (quad ^ d, 0, 0))
        fc_out = jnp.concatenate(
            [
                fc_parts[i][:, j * width : (j + 1) * width]
                for j in range(F)
                for i in range(QUAD)
            ],
            axis=1,
        ).astype(F32)
        out_out = sum_z(out_w_grad)
        query_out = sum_z(query_w_grad)
        kv_sum = keyval_w_grad
        for bit in bits_of(C):
            kv_sum = kv_sum + swk(kv_sum.astype(BF16), bit).astype(F32)

        fc_b_full = lax.dynamic_update_slice(
            jnp.zeros((F, QUAD, width), F32), fc_b_grad.reshape(F, 1, width), (0, quad, 0)
        )

        def sum_vectors(vectors):
            sizes = [v.size // F for v in vectors]
            packed = jnp.concatenate([v.reshape(F, -1) for v in vectors], axis=1)
            packed = jnp.pad(packed, ((0, 0), (0, -packed.shape[1] % 1024)))
            packed = packed.reshape(F, -1, 128)

            def one(d):
                return lax.dynamic_slice(packed, (f ^ d, 0, 0), (1,) + packed.shape[1:])[0]

            total = one(0)
            for d in range(1, F):
                total = total + swap_f(one(d), d, F)
            for bit in bits_of(C):
                total = total + swk(total, bit)
            total = total.reshape(-1)
            outs = []
            at = 0
            for size in sizes:
                outs.append(total[at : at + size])
                at += size
            return outs

        def column_sum(x):
            return jnp.sum(x.astype(F32), axis=0)

        g1, s1, bq, bv, g2, s2, bp, bo, bf = sum_vectors(
            [
                gain_one_grad,
                shift_one_grad,
                behind(column_sum(d_queries), fc_sum),
                column_sum(d_keyvals[:, HD:]),
                gain_two_grad,
                shift_two_grad,
                column_sum(cot_own),
                column_sum(d_branch),
                fc_b_full,
            ]
        )
        return (
            hidden_out, hidden_grad, g1, s1, query_out, bq, kv_sum, bv, out_out, bo, g2, s2,
            fc_out, bf, proj_out, bp,
        )

    return per_device


def solution(mesh):
    tokens = P(None, ("fsdp", "ctx"), None)
    places = P(None, ("fsdp", "ctx"))
    vec = P("fsdp")
    mat = P("fsdp", None)
    grads = (vec, vec, mat, vec, mat, vec, mat, vec, vec, vec, mat, vec, mat, vec)
    return jax.shard_map(
        build(mesh.shape["fsdp"], mesh.shape["ctx"]),
        mesh=mesh,
        in_specs=(tokens, places, places) + grads + (tokens,),
        out_specs=(tokens, tokens) + grads,
        check_vma=False,
    )
```

```python
import functools
import math

import jax
import jax.numpy as jnp
from jax import lax
from jax.experimental import pallas as pl
from jax.experimental.pallas import tpu as pltpu
from jax.sharding import PartitionSpec as P

D = 2048
HEADS = 16
HD = 128
QUAD = 4
F32 = jnp.float32
BF16 = jnp.bfloat16


def layer_norm(values, gain, shift):
    center = jnp.mean(values, axis=-1, keepdims=True)
    shifted = values - center
    spread = jnp.mean(shifted * shifted, axis=-1, keepdims=True)
    return shifted * lax.rsqrt(spread + 1e-05) * gain + shift


def layer_norm_back(values, gain, d_out):
    center = jnp.mean(values, axis=-1, keepdims=True)
    shifted = values - center
    spread = jnp.mean(shifted * shifted, axis=-1, keepdims=True)
    r = lax.rsqrt(spread + 1e-05)
    xhat = shifted * r
    e = d_out * gain
    d_values = r * (
        e - jnp.mean(e, axis=-1, keepdims=True) - xhat * jnp.mean(e * xhat, axis=-1, keepdims=True)
    )
    return d_values, jnp.sum(d_out * xhat, axis=0), jnp.sum(d_out, axis=0)


def gelu_and_slope(u):
    a = math.sqrt(2.0 / math.pi)
    t = jnp.tanh(a * (u + 0.044715 * u * u * u))
    half = 0.5 * (1.0 + t)
    slope = half + 0.5 * u * (1.0 - t * t) * a * (1.0 + 3.0 * 0.044715 * u * u)
    return u * half, slope


def dot(a, b):
    return jnp.dot(a, b, preferred_element_type=F32)


def dot_t(a, b):
    return lax.dot_general(a, b, (((1,), (1,)), ((), ())), preferred_element_type=F32)


def t_dot(a, b):
    return lax.dot_general(a, b, (((0,), (0,)), ((), ())), preferred_element_type=F32)


def swap_f(x, bit, size):
    return lax.ppermute(x, "fsdp", [(i, i ^ bit) for i in range(size)])


def swap_k(x, bit, size):
    return lax.ppermute(x, "ctx", [(i, i ^ bit) for i in range(size)])


def bits_of(size):
    out = []
    bit = 1
    while bit < size:
        out.append(bit)
        bit *= 2
    return out


def flip(index, d):
    bit = 1
    while bit <= d:
        if d & bit:
            index = index + bit * (1 - 2 * ((index // bit) % 2))
        bit *= 2
    return index


def head_kernel(
    F, C, vec_ref, place_ref, wkv_ref, wq_ref, vec_out, place_out, wkv_out, wq_out, send, recv, local
):
    f = lax.axis_index("fsdp")
    k = lax.axis_index("ctx")
    core = k % 2
    barrier = pltpu.get_barrier_semaphore()
    partners = [{"fsdp": flip(f, bit)} for bit in bits_of(F)]
    partners += [{"ctx": flip(k, bit)} for bit in bits_of(C)]
    for partner in partners:
        pl.semaphore_signal(barrier, inc=1, device_id=partner, device_id_type=pl.DeviceIdType.MESH)
    pl.semaphore_wait(barrier, len(partners))

    count = [0]
    started = []

    def remote(src, dst, partner):
        n = count[0]
        count[0] += 1
        copy = pltpu.make_async_remote_copy(
            src_ref=src,
            dst_ref=dst,
            send_sem=send.at[n],
            recv_sem=recv.at[n],
            device_id=partner,
            device_id_type=pl.DeviceIdType.MESH,
        )
        copy.start()
        started.append(copy)
        return copy

    own_copies = []

    def keep(src, dst):
        copy = pltpu.make_async_copy(src, dst, local.at[len(own_copies)])
        copy.start()
        own_copies.append(copy)

    def tree(own, place, order, me, axis, handed=None):
        come = {}

        def sends(d, position):
            for p in range(position, len(order)):
                src = own if d == 0 else place(d, d)
                copy = remote(src, place(d ^ order[p], d), {axis: flip(me, order[p])})
                come[d ^ order[p]] = (copy, p + 1)

        sends(0, 0)
        yield
        done = {0}
        while len(done) < len(come) + 1:
            for d in list(come):
                if d in done:
                    continue
                copy, position = come[d]
                copy.wait_recv()
                done.add(d)
                sends(d, position)
                if handed is not None:
                    handed(place(d, d))
                yield

    vec_rows = vec_ref.shape[0]
    trees = [
        tree(vec_ref, lambda d, e: vec_out.at[flip(f, e)], bits_of(F), f, "fsdp"),
    ]
    keep(vec_ref, vec_out.at[f])
    arrivals = []
    for ref, out in ((wkv_ref, wkv_out), (wq_ref, wq_out)):
        rows, width = ref.shape
        half, wide = rows // 2, width // 2
        columns = pl.ds(pl.multiple_of(core * wide, wide), wide)
        keep(ref, out.at[pl.ds(pl.multiple_of(f * rows, rows), rows)])
        for h, order in enumerate((bits_of(F), bits_of(F)[::-1])):

            def place(d, e, out=out, h=h, rows=rows, half=half, columns=columns):
                start = flip(f, e) * rows + h * half
                return out.at[pl.ds(pl.multiple_of(start, half), half), columns]

            def handed(block):
                arrivals.append(remote(block, block, {"ctx": flip(k, 1)}))

            own = ref.at[pl.ds(h * half, half), columns]
            trees.append(tree(own, place, order, f, "fsdp", handed))
    keep(place_ref, place_out.at[0])
    trees.append(tree(place_ref, lambda d, e: place_out.at[d], bits_of(C)[::-1], k, "ctx"))
    while trees:
        for one in list(trees):
            try:
                next(one)
            except StopIteration:
                trees.remove(one)
    for copy in arrivals:
        copy.wait_recv()
    for copy in started:
        copy.wait_send()
    for copy in own_copies:
        copy.wait()


def gather_head(F, C, vec, place, wkv, wq):
    copies = (F - 1) + (C - 1) + 2 * 2 * 2 * (F - 1)
    return pl.pallas_call(
        functools.partial(head_kernel, F, C),
        in_specs=[pl.BlockSpec(memory_space=pl.ANY)] * 4,
        out_specs=[pl.BlockSpec(memory_space=pl.ANY)] * 4,
        out_shape=[
            jax.ShapeDtypeStruct((F,) + vec.shape, vec.dtype),
            jax.ShapeDtypeStruct((C,) + place.shape, place.dtype),
            jax.ShapeDtypeStruct((F * wkv.shape[0], wkv.shape[1]), wkv.dtype),
            jax.ShapeDtypeStruct((F * wq.shape[0], wq.shape[1]), wq.dtype),
        ],
        scratch_shapes=[
            pltpu.SemaphoreType.DMA((copies,)),
            pltpu.SemaphoreType.DMA((copies,)),
            pltpu.SemaphoreType.DMA((4,)),
        ],
        compiler_params=pltpu.CompilerParams(collective_id=0, has_side_effects=True),
        name="gather_head",
    )(vec, place, wkv, wq)


HEAD_STEP = 2
KEY_STEP = 512


def forward_kernel(scale, q_ref, kv_ref, kplace_ref, qplace_ref, o_ref, lse_ref, bias, vt_ref, sc):
    keys = kv_ref.shape[0]

    @pl.when(pl.program_id(0) == 0)
    def _():
        fill_bias(kplace_ref, qplace_ref, bias)
        for at in range(0, keys, KEY_STEP):
            vt_ref[:, at : at + KEY_STEP] = kv_ref[at : at + KEY_STEP, HD:].T

    for h in range(HEAD_STEP):
        q = q_ref[:, h * HD : (h + 1) * HD]
        peak = None
        for at in range(0, keys, KEY_STEP):
            s = dot_t(kv_ref[at : at + KEY_STEP, :HD], q) * scale + bias[at : at + KEY_STEP]
            sc[h, at : at + KEY_STEP] = s
            top = jnp.max(s, axis=0, keepdims=True)
            peak = top if peak is None else jnp.maximum(peak, top)
        total = jnp.zeros_like(peak)
        acc = jnp.zeros((HD, q.shape[0]), F32)
        for at in range(0, keys, KEY_STEP):
            p = jnp.exp(sc[h, at : at + KEY_STEP] - peak)
            total = total + jnp.sum(p, axis=0, keepdims=True)
            acc = acc + dot(vt_ref[:, at : at + KEY_STEP], p.astype(BF16))
        o_ref[:, h * HD : (h + 1) * HD] = (acc / total).T.astype(BF16)
        lse_ref[0, h : h + 1] = peak + jnp.log(total)


def fill_bias(kplace_ref, qplace_ref, bias):
    for at in range(0, bias.shape[0], KEY_STEP):
        seg_k = kplace_ref[at : at + KEY_STEP, 0:1]
        pos_k = kplace_ref[at : at + KEY_STEP, 1:2]
        seg_q = qplace_ref[0:1]
        pos_q = qplace_ref[1:2]
        seen = (pos_k <= pos_q) & ((seg_k == 0) | (seg_k == seg_q))
        bias[at : at + KEY_STEP] = jnp.where(seen, 0.0, -1e30)


def backward_kernel(
    scale, q_ref, do_ref, o_ref, lse_ref, kv_ref, kplace_ref, qplace_ref, dq_ref, dkv_ref, bias, kt_ref
):
    keys = kv_ref.shape[0]

    @pl.when(pl.program_id(0) == 0)
    def _():
        fill_bias(kplace_ref, qplace_ref, bias)
        dkv_ref[...] = jnp.zeros_like(dkv_ref)
        for at in range(0, keys, KEY_STEP):
            kt_ref[:, at : at + KEY_STEP] = kv_ref[at : at + KEY_STEP, :HD].T

    for h in range(HEAD_STEP):
        q = q_ref[:, h * HD : (h + 1) * HD]
        do = do_ref[:, h * HD : (h + 1) * HD]
        o = o_ref[:, h * HD : (h + 1) * HD]
        inner = jnp.sum((do.astype(F32) * o.astype(F32)).T, axis=0, keepdims=True)
        lse = lse_ref[0, h : h + 1]
        dq = jnp.zeros((HD, q.shape[0]), F32)
        for at in range(0, keys, KEY_STEP):
            rows = slice(at, at + KEY_STEP)
            s = dot_t(kv_ref[rows, :HD], q) * scale + bias[rows]
            p = jnp.exp(s - lse)
            dp = dot_t(kv_ref[rows, HD:], do)
            ds = (p * (dp - inner)).astype(BF16)
            dkv_ref[rows, HD:] += dot(p.astype(BF16), do)
            dkv_ref[rows, :HD] += dot(ds, q)
            dq = dq + dot(kt_ref[:, rows], ds)
        dq_ref[:, h * HD : (h + 1) * HD] = (dq * scale).T.astype(BF16)


def attend_forward(queries, kv, kplace, qplace, scale):
    rows = queries.shape[0]
    keys = kv.shape[0]
    whole = lambda x: pl.BlockSpec(x.shape, lambda h: (0,) * x.ndim)
    heads = pl.BlockSpec((rows, HEAD_STEP * HD), lambda h: (0, h))
    return pl.pallas_call(
        functools.partial(forward_kernel, scale),
        grid=(HEADS // HEAD_STEP,),
        in_specs=[heads, whole(kv), whole(kplace), whole(qplace)],
        out_specs=[heads, pl.BlockSpec((1, HEAD_STEP, rows), lambda h: (h, 0, 0))],
        out_shape=[
            jax.ShapeDtypeStruct((rows, HEADS * HD), BF16),
            jax.ShapeDtypeStruct((HEADS // HEAD_STEP, HEAD_STEP, rows), F32),
        ],
        scratch_shapes=[
            pltpu.VMEM((keys, rows), F32),
            pltpu.VMEM((HD, keys), BF16),
            pltpu.VMEM((HEAD_STEP, keys, rows), F32),
        ],
        compiler_params=pltpu.CompilerParams(vmem_limit_bytes=32 * 1024 * 1024),
        cost_estimate=pl.CostEstimate(
            flops=8 * rows * keys * HEADS * HD,
            bytes_accessed=4 * rows * HEADS * HD,
            transcendentals=rows * keys * HEADS,
        ),
        name="attend_forward",
    )(queries, kv, kplace, qplace)


def attend_backward(queries, d_mixed, mixed, lse, kv, kplace, qplace, scale):
    rows = queries.shape[0]
    keys = kv.shape[0]
    whole = lambda x: pl.BlockSpec(x.shape, lambda h: (0,) * x.ndim)
    heads = pl.BlockSpec((rows, HEAD_STEP * HD), lambda h: (0, h))
    return pl.pallas_call(
        functools.partial(backward_kernel, scale),
        grid=(HEADS // HEAD_STEP,),
        in_specs=[
            heads,
            heads,
            heads,
            pl.BlockSpec((1, HEAD_STEP, rows), lambda h: (h, 0, 0)),
            whole(kv),
            whole(kplace),
            whole(qplace),
        ],
        out_specs=[heads, pl.BlockSpec((keys, 2 * HD), lambda h: (0, 0))],
        out_shape=[
            jax.ShapeDtypeStruct((rows, HEADS * HD), BF16),
            jax.ShapeDtypeStruct((keys, 2 * HD), F32),
        ],
        scratch_shapes=[pltpu.VMEM((keys, rows), F32), pltpu.VMEM((HD, keys), BF16)],
        compiler_params=pltpu.CompilerParams(vmem_limit_bytes=32 * 1024 * 1024),
        cost_estimate=pl.CostEstimate(
            flops=18 * rows * keys * HEADS * HD,
            bytes_accessed=8 * rows * HEADS * HD,
            transcendentals=rows * keys * HEADS,
        ),
        name="attend_backward",
    )(queries, d_mixed, mixed, lse, kv, kplace, qplace)


def build(F, C):
    Z = C // 2

    def per_device(
        hidden_in,
        segment_ids,
        positions,
        norm1_gain,
        norm1_bias,
        query_weight,
        query_bias,
        keyval_weight,
        value_bias,
        out_weight,
        out_bias,
        norm2_gain,
        norm2_bias,
        fc_weight,
        fc_bias,
        proj_weight,
        proj_bias,
        out_grad,
    ):
        micros, rows = hidden_in.shape[:2]
        tok = micros * rows
        scale = 1.0 / math.sqrt(HD)
        f = lax.axis_index("fsdp")
        k = lax.axis_index("ctx")
        core = k % 2
        quad = k % QUAD
        zi = k // 2
        hsh = D // F
        width = fc_weight.shape[1] // F // QUAD

        def pick_core(a, b):
            return jnp.where(core == 0, a, b)

        def in_order(own, other):
            return pick_core(
                jnp.concatenate([own, other], axis=1), jnp.concatenate([other, own], axis=1)
            )

        def halves(x):
            w = x.shape[1] // 2
            return pick_core(x[:, :w], x[:, w:]), pick_core(x[:, w:], x[:, :w])

        def after(x, *deps):
            return lax.optimization_barrier((x,) + deps)[0]

        def behind(x, *deps):
            zero = sum(
                jnp.minimum(jnp.abs(d[(slice(0, 1),) * d.ndim].reshape(()).astype(F32)), 0.0)
                for d in deps
            )
            return (x.astype(F32) + zero).astype(x.dtype)

        def swk(x, bit):
            return swap_k(x, bit, C)

        def gather_ctx(x):
            held = {0: x}
            for bit in bits_of(C)[1:][::-1] + [1]:
                for d in list(held):
                    held[d ^ bit] = swk(held[d], bit)
            return [held[d] for d in range(C)]

        def gather_quad(x):
            a = swk(x, 1)
            b = swk(x, 2)
            c = swk(b, 1)
            return [x, b, a, c]

        names = (
            norm1_gain, norm1_bias, query_bias, out_bias, norm2_gain, norm2_bias, proj_bias,
            fc_bias, value_bias,
        )
        sizes = [v.shape[0] for v in names]
        packed = jnp.concatenate(names)
        pad = -packed.shape[0] % 2048
        packed = jnp.pad(packed, (0, pad)).reshape(-1, 128)
        places = jnp.concatenate([segment_ids, positions], axis=0)
        vec, places, w_keyval, w_query = gather_head(
            F, C, packed, places, keyval_weight, query_weight
        )
        vec = vec.reshape(F, -1).astype(F32)
        full = []
        at = 0
        for size in sizes:
            full.append(vec[:, at : at + size])
            at += size
        gain_one, shift_one, b_query, b_out, gain_two, shift_two, b_proj = [
            v.reshape(-1) for v in full[:7]
        ]
        b_value = full[8].reshape(-1)
        b_fc = lax.dynamic_slice(
            full[7].reshape(F, QUAD, width), (0, quad, 0), (F, 1, width)
        ).reshape(-1)
        kv_bias = jnp.concatenate([jnp.zeros((HD,), F32), b_value])

        seg_all = [places[:, m].reshape(-1) for m in range(micros)]
        pos_all = [places[:, micros + m].reshape(-1) for m in range(micros)]

        wo_own = lax.all_gather(halves(out_weight)[0], "fsdp", axis=0, tiled=True)
        wo_other = swk(wo_own, 1)

        fc_piece = jnp.concatenate(
            [
                lax.dynamic_slice(fc_weight, (0, (j * QUAD + quad) * width), (hsh, width))
                for j in range(F)
            ],
            axis=1,
        )
        proj_piece = lax.dynamic_slice(proj_weight, (quad * width, 0), (width, D))
        w_fc = lax.all_gather(fc_piece, "fsdp", axis=0, tiled=True)
        w_proj = lax.all_gather(proj_piece, "fsdp", axis=0, tiled=True)

        hidden = hidden_in.reshape(tok, D).astype(F32)
        normed1 = layer_norm(hidden, gain_one, shift_one).astype(BF16)
        keyvals = (dot(normed1, w_keyval) + kv_bias).astype(BF16)
        group_kv = jnp.concatenate(
            gather_ctx(keyvals.reshape(micros, rows, 2 * HD)), axis=1
        )
        queries = (dot(normed1, w_query) + b_query).astype(BF16)
        kplace = [jnp.stack([seg_all[m], pos_all[m]], axis=1) for m in range(micros)]
        qplace = [jnp.stack([segment_ids[m], positions[m]]) for m in range(micros)]
        queries = [queries[m * rows : (m + 1) * rows] for m in range(micros)]
        mixed = []
        lse = []
        middle = []
        normed2_blocks = []
        for m in range(micros):
            mix, lse_rows = attend_forward(
                queries[m], group_kv[m], kplace[m], qplace[m], scale
            )
            mixed.append(mix)
            lse.append(lse_rows)
            mid = (
                hidden[m * rows : (m + 1) * rows]
                + in_order(dot(mix, wo_own), dot(mix, wo_other))
                + b_out
            )
            middle.append(mid)
            normed2_own = layer_norm(mid, gain_two, shift_two).astype(BF16)
            normed2_blocks.append(gather_quad(normed2_own))
            if m + 1 < micros:
                queries[m + 1] = behind(queries[m + 1], normed2_own)
        all_mixed = jnp.concatenate(mixed, axis=0)
        middle = jnp.concatenate(middle, axis=0)
        normed2 = jnp.concatenate(
            [normed2_blocks[m][d] for d in range(QUAD) for m in range(micros)], axis=0
        )
        cot_own = out_grad.reshape(tok, D)
        cot = jnp.concatenate(gather_quad(after(cot_own, group_kv)), axis=0)

        active, slope = gelu_and_slope(dot(normed2, w_fc) + b_fc)
        active = active.astype(BF16)
        slope = slope.astype(BF16)

        def scatter(term):
            return lax.psum_scatter(term, "fsdp", scatter_dimension=0, tiled=True)

        def ffn_grad(left, right):
            term = t_dot(left, right).astype(BF16)
            return lax.psum_scatter(term, "fsdp", scatter_dimension=0, tiled=True), term

        proj_grad, proj_term = ffn_grad(active, cot)

        def reduce_quad(x, product):
            got = swk(product(x[2 * tok :]).astype(BF16), 1).astype(F32)
            passed = (product(x[tok : 2 * tok]) + got[tok:]).astype(BF16)
            own = product(x[:tok]) + got[:tok]
            return [swk(passed[m * rows : (m + 1) * rows], 2) for m in range(micros)], passed, own

        d_before = (dot_t(after(cot, proj_term), w_proj) * slope.astype(F32)).astype(BF16)
        came, passed, own = reduce_quad(d_before, lambda x: dot_t(x, w_fc))
        d_normed2 = own + jnp.concatenate(came).astype(F32)
        fc_grad, fc_term = ffn_grad(after(normed2, passed), d_before)
        fc_b_grad = jnp.sum(d_before.astype(F32), axis=0)

        def across_quads(x, parts):
            size = x.shape[0] // parts
            outs = []
            for i in range(parts):
                block = x[i * size : (i + 1) * size]
                if i:
                    block = behind(block, outs[-1])
                for bit in bits_of(C)[2:]:
                    block = (block.astype(F32) + swk(block, bit).astype(F32)).astype(BF16)
                outs.append(block)
            return outs

        proj_sums = across_quads(proj_grad, 4)
        ffn, ffn_passed, ffn_own = reduce_quad(after(active, fc_term), lambda x: dot(x, w_proj))

        d_middle, gain_two_grad, shift_two_grad = layer_norm_back(
            behind(middle, proj_sums[0], ffn_passed, ffn_own), gain_two, d_normed2
        )
        d_middle = cot_own.astype(F32) + d_middle
        d_branch = d_middle.astype(BF16)
        branch_own, branch_other = halves(d_branch)
        d_mixed = (dot_t(branch_own, wo_own) + dot_t(branch_other, wo_other)).astype(BF16)
        d_mixed = [d_mixed[m * rows : (m + 1) * rows] for m in range(micros)]
        kv_scale = jnp.concatenate([jnp.full((HD,), scale, F32), jnp.ones((HD,), F32)])
        d_queries = []
        kv_terms = []
        for m in range(micros):
            d_mixed[m] = behind(d_mixed[m], proj_sums[m + 1], *d_queries)
            dq, dkv = attend_backward(
                queries[m], d_mixed[m], mixed[m], lse[m], group_kv[m], kplace[m], qplace[m], scale
            )
            d_queries.append(dq)
            kv_terms.append(dkv)
        d_queries = jnp.concatenate(d_queries, axis=0)
        dq_own, dq_other = halves(behind(d_queries, proj_sums[3]))
        dq_pair = jnp.concatenate([dq_own, swk(dq_other, 1)], axis=0)
        normed1_pair = jnp.concatenate([normed1, swk(normed1, 1)], axis=0)
        query_term = t_dot(normed1_pair, dq_pair).astype(BF16)
        query_w_grad = scatter(query_term)
        branch_own, branch_other = halves(behind(d_branch, query_term))
        branch_pair = jnp.concatenate([branch_own, swk(branch_other, 1)], axis=0)
        mixed_pair = jnp.concatenate([all_mixed, swk(all_mixed, 1)], axis=0)
        out_term = t_dot(mixed_pair, branch_pair).astype(BF16)
        terms = jnp.stack(kv_terms) * behind(kv_scale, out_term)
        terms = terms.reshape(micros, C, rows, 2 * HD)
        terms = {d: terms[:, d] for d in range(C)}
        for bit in [1] + bits_of(C)[1:][::-1]:
            sent = [d for d in terms if d & bit]
            got = swk(jnp.stack([terms[d] for d in sent]).astype(BF16), bit)
            for i, d in enumerate(sent):
                terms[d ^ bit] = terms[d ^ bit] + got[i].astype(F32)
                del terms[d]
        d_keyvals = terms[0].astype(BF16).reshape(tok, 2 * HD)
        fc_came = swk(behind(fc_grad, d_keyvals), QUAD)
        dkv_own, dkv_other = halves(d_keyvals)
        dkv_pair = jnp.concatenate([dkv_own, swk(dkv_other, 1)], axis=0)
        keyval_term = t_dot(normed1_pair, dkv_pair).astype(BF16)
        out_w_grad = scatter(jnp.concatenate([out_term, keyval_term], axis=1))
        d_normed1 = (
            dot_t(d_queries, w_query) + dot_t(d_keyvals, w_keyval)
        )
        d_hidden, gain_one_grad, shift_one_grad = layer_norm_back(hidden, gain_one, d_normed1)
        hidden_grad = (d_middle + d_hidden).reshape(micros, rows, D)

        ffn = jnp.concatenate([behind(x, hidden_grad) for x in ffn]).astype(F32)
        result = middle + ffn_own + ffn + b_proj
        hidden_out = result.astype(BF16).reshape(micros, rows, D)

        fc_sum = (behind(fc_grad, hidden_grad, query_w_grad).astype(F32) + fc_came.astype(F32)).astype(BF16)
        for bit in bits_of(C)[3:]:
            fc_sum = (fc_sum.astype(F32) + swk(fc_sum, bit).astype(F32)).astype(BF16)

        def reduce_z(x):
            part = x.shape[0] // Z
            blocks = x.astype(BF16).reshape(Z, part, x.shape[1])
            terms = [
                lax.dynamic_slice(blocks, (zi ^ d, 0, 0), (1,) + blocks.shape[1:])[0].astype(F32)
                for d in range(Z)
            ]
            terms = dict(enumerate(terms))
            for bit in bits_of(Z):
                sent = [d for d in terms if d & bit]
                got = swk(jnp.concatenate([terms[d] for d in sent]).astype(BF16), 2 * bit)
                for i, d in enumerate(sent):
                    terms[d ^ bit] = terms[d ^ bit] + got[i * part : (i + 1) * part].astype(F32)
                    del terms[d]
            return terms[0].astype(BF16)

        def expand_z(held):
            part, n = held.shape
            ids = [0]
            for bit in bits_of(Z)[::-1]:
                held = jnp.concatenate([held, swk(held, 2 * bit)])
                ids = ids + [d ^ bit for d in ids]
            out = jnp.full((Z, part, n), 0.125, BF16)
            for i, d in enumerate(ids):
                block = held[i * part : (i + 1) * part]
                out = lax.dynamic_update_slice(out, block[None], (zi ^ d, 0, 0))
            own = out.reshape(Z * part, n)
            return own, swk(own, 1)

        query_block = reduce_z(query_w_grad)
        out_block = reduce_z(out_w_grad)

        members = (0, 2, 1, 3)
        proj_out = jnp.full((QUAD * width, D), 1.0, F32)
        for d, part in zip(members, gather_quad(behind(jnp.concatenate(proj_sums), d_keyvals))):
            proj_out = lax.dynamic_update_slice(proj_out, part.astype(F32), ((quad ^ d) * width, 0))
        fc_parts = jnp.full((QUAD, hsh, F * width), 0.75, BF16)
        fc_blocks = gather_quad(behind(fc_sum, query_block, out_block))
        for d, part in zip(members, fc_blocks):
            fc_parts = lax.dynamic_update_slice(fc_parts, part[None], (quad ^ d, 0, 0))
        fc_out = jnp.concatenate(
            [
                fc_parts[i][:, j * width : (j + 1) * width]
                for j in range(F)
                for i in range(QUAD)
            ],
            axis=1,
        ).astype(F32)
        query_out = in_order(*expand_z(query_block)).astype(F32)
        own, other = expand_z(out_block)
        half = D // 2
        out_out = in_order(own[:, :half], other[:, :half]).astype(F32)
        kv_sum = in_order(own[:, half:], other[:, half:]).astype(F32)

        fc_b_full = lax.dynamic_update_slice(
            jnp.zeros((F, QUAD, width), F32), fc_b_grad.reshape(F, 1, width), (0, quad, 0)
        )

        def sum_vectors(vectors):
            sizes = [v.size // F for v in vectors]
            packed = jnp.concatenate([v.reshape(F, -1) for v in vectors], axis=1)
            packed = jnp.pad(packed, ((0, 0), (0, -packed.shape[1] % 1024)))
            packed = packed.reshape(F, -1, 128)

            def one(d):
                return lax.dynamic_slice(packed, (f ^ d, 0, 0), (1,) + packed.shape[1:])[0]

            total = one(0)
            for d in range(1, F):
                total = total + swap_f(one(d), d, F)
            for bit in bits_of(C):
                total = total + swk(total, bit)
            total = total.reshape(-1)
            outs = []
            at = 0
            for size in sizes:
                outs.append(total[at : at + size])
                at += size
            return outs

        def column_sum(x):
            return jnp.sum(x.astype(F32), axis=0)

        g1, s1, bq, bv, g2, s2, bp, bo, bf = sum_vectors(
            [
                gain_one_grad,
                shift_one_grad,
                behind(column_sum(d_queries), fc_blocks[1]),
                column_sum(d_keyvals[:, HD:]),
                gain_two_grad,
                shift_two_grad,
                column_sum(cot_own),
                column_sum(d_branch),
                fc_b_full,
            ]
        )
        return (
            hidden_out, hidden_grad, g1, s1, query_out, bq, kv_sum, bv, out_out, bo, g2, s2,
            fc_out, bf, proj_out, bp,
        )

    return per_device


def solution(mesh):
    tokens = P(None, ("fsdp", "ctx"), None)
    places = P(None, ("fsdp", "ctx"))
    vec = P("fsdp")
    mat = P("fsdp", None)
    grads = (vec, vec, mat, vec, mat, vec, mat, vec, vec, vec, mat, vec, mat, vec)
    return jax.shard_map(
        build(mesh.shape["fsdp"], mesh.shape["ctx"]),
        mesh=mesh,
        in_specs=(tokens, places, places) + grads + (tokens,),
        out_specs=(tokens, tokens) + grads,
        check_vma=False,
    )
```

```python
import functools
import math

import jax
import jax.numpy as jnp
from jax import lax
from jax.experimental import pallas as pl
from jax.experimental.pallas import tpu as pltpu
from jax.sharding import PartitionSpec as P

D = 2048
HEADS = 16
HD = 128
QUAD = 4
F32 = jnp.float32
BF16 = jnp.bfloat16


def layer_norm(values, gain, shift):
    center = jnp.mean(values, axis=-1, keepdims=True)
    shifted = values - center
    spread = jnp.mean(shifted * shifted, axis=-1, keepdims=True)
    return shifted * lax.rsqrt(spread + 1e-05) * gain + shift


def layer_norm_back(values, gain, d_out):
    center = jnp.mean(values, axis=-1, keepdims=True)
    shifted = values - center
    spread = jnp.mean(shifted * shifted, axis=-1, keepdims=True)
    r = lax.rsqrt(spread + 1e-05)
    xhat = shifted * r
    e = d_out * gain
    d_values = r * (
        e - jnp.mean(e, axis=-1, keepdims=True) - xhat * jnp.mean(e * xhat, axis=-1, keepdims=True)
    )
    return d_values, jnp.sum(d_out * xhat, axis=0), jnp.sum(d_out, axis=0)


def gelu_and_slope(u):
    a = math.sqrt(2.0 / math.pi)
    t = jnp.tanh(a * (u + 0.044715 * u * u * u))
    half = 0.5 * (1.0 + t)
    slope = half + 0.5 * u * (1.0 - t * t) * a * (1.0 + 3.0 * 0.044715 * u * u)
    return u * half, slope


def dot(a, b):
    return jnp.dot(a, b, preferred_element_type=F32)


def dot_t(a, b):
    return lax.dot_general(a, b, (((1,), (1,)), ((), ())), preferred_element_type=F32)


def t_dot(a, b):
    return lax.dot_general(a, b, (((0,), (0,)), ((), ())), preferred_element_type=F32)


def swap_f(x, bit, size):
    return lax.ppermute(x, "fsdp", [(i, i ^ bit) for i in range(size)])


def swap_k(x, bit, size):
    return lax.ppermute(x, "ctx", [(i, i ^ bit) for i in range(size)])


def bits_of(size):
    out = []
    bit = 1
    while bit < size:
        out.append(bit)
        bit *= 2
    return out


def flip(index, d):
    bit = 1
    while bit <= d:
        if d & bit:
            index = index + bit * (1 - 2 * ((index // bit) % 2))
        bit *= 2
    return index


def head_kernel(
    F, C, vec_ref, place_ref, wkv_ref, wq_ref, vec_out, place_out, wkv_out, wq_out, send, recv, local
):
    f = lax.axis_index("fsdp")
    k = lax.axis_index("ctx")
    core = k % 2
    barrier = pltpu.get_barrier_semaphore()
    partners = [{"fsdp": flip(f, bit)} for bit in bits_of(F)]
    partners += [{"ctx": flip(k, bit)} for bit in bits_of(C)]
    for partner in partners:
        pl.semaphore_signal(barrier, inc=1, device_id=partner, device_id_type=pl.DeviceIdType.MESH)
    pl.semaphore_wait(barrier, len(partners))

    count = [0]
    started = []

    def remote(src, dst, partner):
        n = count[0]
        count[0] += 1
        copy = pltpu.make_async_remote_copy(
            src_ref=src,
            dst_ref=dst,
            send_sem=send.at[n],
            recv_sem=recv.at[n],
            device_id=partner,
            device_id_type=pl.DeviceIdType.MESH,
        )
        copy.start()
        started.append(copy)
        return copy

    own_copies = []

    def keep(src, dst):
        copy = pltpu.make_async_copy(src, dst, local.at[len(own_copies)])
        copy.start()
        own_copies.append(copy)

    def tree(own, place, order, me, axis, handed=None):
        come = {}

        def sends(d, position):
            for p in range(position, len(order)):
                src = own if d == 0 else place(d, d)
                copy = remote(src, place(d ^ order[p], d), {axis: flip(me, order[p])})
                come[d ^ order[p]] = (copy, p + 1)

        sends(0, 0)
        yield
        done = {0}
        while len(done) < len(come) + 1:
            for d in list(come):
                if d in done:
                    continue
                copy, position = come[d]
                copy.wait_recv()
                done.add(d)
                sends(d, position)
                if handed is not None:
                    handed(place(d, d))
                yield

    vec_rows = vec_ref.shape[0]
    trees = [
        tree(vec_ref, lambda d, e: vec_out.at[flip(f, e)], bits_of(F), f, "fsdp"),
    ]
    keep(vec_ref, vec_out.at[f])
    arrivals = []
    for ref, out in ((wkv_ref, wkv_out), (wq_ref, wq_out)):
        rows, width = ref.shape
        half, wide = rows // 2, width // 2
        columns = pl.ds(pl.multiple_of(core * wide, wide), wide)
        keep(ref, out.at[pl.ds(pl.multiple_of(f * rows, rows), rows)])
        for h, order in enumerate((bits_of(F), bits_of(F)[::-1])):

            def place(d, e, out=out, h=h, rows=rows, half=half, columns=columns):
                start = flip(f, e) * rows + h * half
                return out.at[pl.ds(pl.multiple_of(start, half), half), columns]

            def handed(block):
                arrivals.append(remote(block, block, {"ctx": flip(k, 1)}))

            own = ref.at[pl.ds(h * half, half), columns]
            trees.append(tree(own, place, order, f, "fsdp", handed))
    keep(place_ref, place_out.at[0])
    trees.append(tree(place_ref, lambda d, e: place_out.at[d], bits_of(C)[::-1], k, "ctx"))
    while trees:
        for one in list(trees):
            try:
                next(one)
            except StopIteration:
                trees.remove(one)
    for copy in arrivals:
        copy.wait_recv()
    for copy in started:
        copy.wait_send()
    for copy in own_copies:
        copy.wait()


def gather_head(F, C, vec, place, wkv, wq):
    copies = (F - 1) + (C - 1) + 2 * 2 * 2 * (F - 1)
    return pl.pallas_call(
        functools.partial(head_kernel, F, C),
        in_specs=[pl.BlockSpec(memory_space=pl.ANY)] * 4,
        out_specs=[pl.BlockSpec(memory_space=pl.ANY)] * 4,
        out_shape=[
            jax.ShapeDtypeStruct((F,) + vec.shape, vec.dtype),
            jax.ShapeDtypeStruct((C,) + place.shape, place.dtype),
            jax.ShapeDtypeStruct((F * wkv.shape[0], wkv.shape[1]), wkv.dtype),
            jax.ShapeDtypeStruct((F * wq.shape[0], wq.shape[1]), wq.dtype),
        ],
        scratch_shapes=[
            pltpu.SemaphoreType.DMA((copies,)),
            pltpu.SemaphoreType.DMA((copies,)),
            pltpu.SemaphoreType.DMA((4,)),
        ],
        compiler_params=pltpu.CompilerParams(collective_id=0, has_side_effects=True),
        name="gather_head",
    )(vec, place, wkv, wq)


HEAD_STEP = 2
KEY_STEP = 512


def forward_kernel(scale, q_ref, kv_ref, kplace_ref, qplace_ref, o_ref, lse_ref, bias, vt_ref, sc):
    keys = kv_ref.shape[0]

    @pl.when(pl.program_id(0) == 0)
    def _():
        fill_bias(kplace_ref, qplace_ref, bias)
        for at in range(0, keys, KEY_STEP):
            vt_ref[:, at : at + KEY_STEP] = kv_ref[at : at + KEY_STEP, HD:].T

    for h in range(HEAD_STEP):
        q = q_ref[:, h * HD : (h + 1) * HD]
        peak = None
        for at in range(0, keys, KEY_STEP):
            s = dot_t(kv_ref[at : at + KEY_STEP, :HD], q) * scale + bias[at : at + KEY_STEP]
            sc[h, at : at + KEY_STEP] = s
            top = jnp.max(s, axis=0, keepdims=True)
            peak = top if peak is None else jnp.maximum(peak, top)
        total = jnp.zeros_like(peak)
        acc = jnp.zeros((HD, q.shape[0]), F32)
        for at in range(0, keys, KEY_STEP):
            p = jnp.exp(sc[h, at : at + KEY_STEP] - peak)
            total = total + jnp.sum(p, axis=0, keepdims=True)
            acc = acc + dot(vt_ref[:, at : at + KEY_STEP], p.astype(BF16))
        o_ref[:, h * HD : (h + 1) * HD] = (acc / total).T.astype(BF16)
        lse_ref[0, h : h + 1] = peak + jnp.log(total)


def fill_bias(kplace_ref, qplace_ref, bias):
    for at in range(0, bias.shape[0], KEY_STEP):
        seg_k = kplace_ref[at : at + KEY_STEP, 0:1]
        pos_k = kplace_ref[at : at + KEY_STEP, 1:2]
        seg_q = qplace_ref[0:1]
        pos_q = qplace_ref[1:2]
        seen = (pos_k <= pos_q) & ((seg_k == 0) | (seg_k == seg_q))
        bias[at : at + KEY_STEP] = jnp.where(seen, 0.0, -1e30)


def backward_kernel(
    scale, q_ref, do_ref, o_ref, lse_ref, kv_ref, kplace_ref, qplace_ref, dq_ref, dkv_ref, bias, kt_ref
):
    keys = kv_ref.shape[0]

    @pl.when(pl.program_id(0) == 0)
    def _():
        fill_bias(kplace_ref, qplace_ref, bias)
        dkv_ref[...] = jnp.zeros_like(dkv_ref)
        for at in range(0, keys, KEY_STEP):
            kt_ref[:, at : at + KEY_STEP] = kv_ref[at : at + KEY_STEP, :HD].T

    for h in range(HEAD_STEP):
        q = q_ref[:, h * HD : (h + 1) * HD]
        do = do_ref[:, h * HD : (h + 1) * HD]
        o = o_ref[:, h * HD : (h + 1) * HD]
        inner = jnp.sum((do.astype(F32) * o.astype(F32)).T, axis=0, keepdims=True)
        lse = lse_ref[0, h : h + 1]
        dq = jnp.zeros((HD, q.shape[0]), F32)
        for at in range(0, keys, KEY_STEP):
            rows = slice(at, at + KEY_STEP)
            s = dot_t(kv_ref[rows, :HD], q) * scale + bias[rows]
            p = jnp.exp(s - lse)
            dp = dot_t(kv_ref[rows, HD:], do)
            ds = (p * (dp - inner)).astype(BF16)
            dkv_ref[rows, HD:] += dot(p.astype(BF16), do)
            dkv_ref[rows, :HD] += dot(ds, q)
            dq = dq + dot(kt_ref[:, rows], ds)
        dq_ref[:, h * HD : (h + 1) * HD] = (dq * scale).T.astype(BF16)


def attend_forward(queries, kv, kplace, qplace, scale):
    rows = queries.shape[0]
    keys = kv.shape[0]
    whole = lambda x: pl.BlockSpec(x.shape, lambda h: (0,) * x.ndim)
    heads = pl.BlockSpec((rows, HEAD_STEP * HD), lambda h: (0, h))
    return pl.pallas_call(
        functools.partial(forward_kernel, scale),
        grid=(HEADS // HEAD_STEP,),
        in_specs=[heads, whole(kv), whole(kplace), whole(qplace)],
        out_specs=[heads, pl.BlockSpec((1, HEAD_STEP, rows), lambda h: (h, 0, 0))],
        out_shape=[
            jax.ShapeDtypeStruct((rows, HEADS * HD), BF16),
            jax.ShapeDtypeStruct((HEADS // HEAD_STEP, HEAD_STEP, rows), F32),
        ],
        scratch_shapes=[
            pltpu.VMEM((keys, rows), F32),
            pltpu.VMEM((HD, keys), BF16),
            pltpu.VMEM((HEAD_STEP, keys, rows), F32),
        ],
        compiler_params=pltpu.CompilerParams(vmem_limit_bytes=32 * 1024 * 1024),
        cost_estimate=pl.CostEstimate(
            flops=8 * rows * keys * HEADS * HD,
            bytes_accessed=4 * rows * HEADS * HD,
            transcendentals=rows * keys * HEADS,
        ),
        name="attend_forward",
    )(queries, kv, kplace, qplace)


def attend_backward(queries, d_mixed, mixed, lse, kv, kplace, qplace, scale):
    rows = queries.shape[0]
    keys = kv.shape[0]
    whole = lambda x: pl.BlockSpec(x.shape, lambda h: (0,) * x.ndim)
    heads = pl.BlockSpec((rows, HEAD_STEP * HD), lambda h: (0, h))
    return pl.pallas_call(
        functools.partial(backward_kernel, scale),
        grid=(HEADS // HEAD_STEP,),
        in_specs=[
            heads,
            heads,
            heads,
            pl.BlockSpec((1, HEAD_STEP, rows), lambda h: (h, 0, 0)),
            whole(kv),
            whole(kplace),
            whole(qplace),
        ],
        out_specs=[heads, pl.BlockSpec((keys, 2 * HD), lambda h: (0, 0))],
        out_shape=[
            jax.ShapeDtypeStruct((rows, HEADS * HD), BF16),
            jax.ShapeDtypeStruct((keys, 2 * HD), F32),
        ],
        scratch_shapes=[pltpu.VMEM((keys, rows), F32), pltpu.VMEM((HD, keys), BF16)],
        compiler_params=pltpu.CompilerParams(vmem_limit_bytes=32 * 1024 * 1024),
        cost_estimate=pl.CostEstimate(
            flops=18 * rows * keys * HEADS * HD,
            bytes_accessed=8 * rows * HEADS * HD,
            transcendentals=rows * keys * HEADS,
        ),
        name="attend_backward",
    )(queries, d_mixed, mixed, lse, kv, kplace, qplace)


def build(F, C):
    Z = C // 2

    def per_device(
        hidden_in,
        segment_ids,
        positions,
        norm1_gain,
        norm1_bias,
        query_weight,
        query_bias,
        keyval_weight,
        value_bias,
        out_weight,
        out_bias,
        norm2_gain,
        norm2_bias,
        fc_weight,
        fc_bias,
        proj_weight,
        proj_bias,
        out_grad,
    ):
        micros, rows = hidden_in.shape[:2]
        tok = micros * rows
        scale = 1.0 / math.sqrt(HD)
        f = lax.axis_index("fsdp")
        k = lax.axis_index("ctx")
        core = k % 2
        quad = k % QUAD
        zi = k // 2
        hsh = D // F
        width = fc_weight.shape[1] // F // QUAD

        def pick_core(a, b):
            return jnp.where(core == 0, a, b)

        def in_order(own, other):
            return pick_core(
                jnp.concatenate([own, other], axis=1), jnp.concatenate([other, own], axis=1)
            )

        def halves(x):
            w = x.shape[1] // 2
            return pick_core(x[:, :w], x[:, w:]), pick_core(x[:, w:], x[:, :w])

        def after(x, *deps):
            return lax.optimization_barrier((x,) + deps)[0]

        def behind(x, *deps):
            zero = sum(
                jnp.minimum(jnp.abs(d[(slice(0, 1),) * d.ndim].reshape(()).astype(F32)), 0.0)
                for d in deps
            )
            return (x.astype(F32) + zero).astype(x.dtype)

        def swk(x, bit):
            return swap_k(x, bit, C)

        def gather_ctx(x):
            held = {0: x}
            for bit in bits_of(C)[1:][::-1] + [1]:
                for d in list(held):
                    held[d ^ bit] = swk(held[d], bit)
            return [held[d] for d in range(C)]

        def gather_quad(x):
            a = swk(x, 1)
            b = swk(x, 2)
            c = swk(b, 1)
            return [x, b, a, c]

        names = (
            norm1_gain, norm1_bias, query_bias, out_bias, norm2_gain, norm2_bias, proj_bias,
            fc_bias, value_bias,
        )
        sizes = [v.shape[0] for v in names]
        packed = jnp.concatenate(names)
        pad = -packed.shape[0] % 2048
        packed = jnp.pad(packed, (0, pad)).reshape(-1, 128)
        places = jnp.concatenate([segment_ids, positions], axis=0)
        vec, places, w_keyval, w_query = gather_head(
            F, C, packed, places, keyval_weight, query_weight
        )
        vec = vec.reshape(F, -1).astype(F32)
        full = []
        at = 0
        for size in sizes:
            full.append(vec[:, at : at + size])
            at += size
        gain_one, shift_one, b_query, b_out, gain_two, shift_two, b_proj = [
            v.reshape(-1) for v in full[:7]
        ]
        b_value = full[8].reshape(-1)
        b_fc = lax.dynamic_slice(
            full[7].reshape(F, QUAD, width), (0, quad, 0), (F, 1, width)
        ).reshape(-1)
        kv_bias = jnp.concatenate([jnp.zeros((HD,), F32), b_value])

        seg_all = [places[:, m].reshape(-1) for m in range(micros)]
        pos_all = [places[:, micros + m].reshape(-1) for m in range(micros)]

        wo_own = lax.all_gather(halves(out_weight)[0], "fsdp", axis=0, tiled=True)
        wo_other = swk(wo_own, 1)

        fc_piece = jnp.concatenate(
            [
                lax.dynamic_slice(fc_weight, (0, (j * QUAD + quad) * width), (hsh, width))
                for j in range(F)
            ],
            axis=1,
        )
        proj_piece = lax.dynamic_slice(proj_weight, (quad * width, 0), (width, D))
        w_fc = lax.all_gather(fc_piece, "fsdp", axis=0, tiled=True)
        w_proj = lax.all_gather(proj_piece, "fsdp", axis=0, tiled=True)

        hidden = hidden_in.reshape(tok, D).astype(F32)
        normed1 = layer_norm(hidden, gain_one, shift_one).astype(BF16)
        keyvals = (dot(normed1, w_keyval) + kv_bias).astype(BF16)
        group_kv = jnp.concatenate(
            gather_ctx(keyvals.reshape(micros, rows, 2 * HD)), axis=1
        )
        queries = (dot(normed1, w_query) + b_query).astype(BF16)
        kplace = [jnp.stack([seg_all[m], pos_all[m]], axis=1) for m in range(micros)]
        qplace = [jnp.stack([segment_ids[m], positions[m]]) for m in range(micros)]
        queries = [queries[m * rows : (m + 1) * rows] for m in range(micros)]
        mixed = []
        lse = []
        middle = []
        normed2_blocks = []
        for m in range(micros):
            mix, lse_rows = attend_forward(
                queries[m], group_kv[m], kplace[m], qplace[m], scale
            )
            mixed.append(mix)
            lse.append(lse_rows)
            mid = (
                hidden[m * rows : (m + 1) * rows]
                + in_order(dot(mix, wo_own), dot(mix, wo_other))
                + b_out
            )
            middle.append(mid)
            normed2_own = layer_norm(mid, gain_two, shift_two).astype(BF16)
            normed2_blocks.append(gather_quad(normed2_own))
            if m + 1 < micros:
                queries[m + 1] = behind(queries[m + 1], normed2_own)
        all_mixed = jnp.concatenate(mixed, axis=0)
        middle = jnp.concatenate(middle, axis=0)
        normed2 = jnp.concatenate(
            [normed2_blocks[m][d] for d in range(QUAD) for m in range(micros)], axis=0
        )
        cot_own = out_grad.reshape(tok, D)
        cot = jnp.concatenate(gather_quad(after(cot_own, group_kv)), axis=0)

        active, slope = gelu_and_slope(dot(normed2, w_fc) + b_fc)
        active = active.astype(BF16)
        slope = slope.astype(BF16)

        def scatter(term):
            return lax.psum_scatter(term, "fsdp", scatter_dimension=0, tiled=True)

        def ffn_grad(left, right):
            term = t_dot(left, right).astype(BF16)
            return lax.psum_scatter(term, "fsdp", scatter_dimension=0, tiled=True), term

        proj_grad, proj_term = ffn_grad(active, cot)

        def reduce_quad(x, product):
            got = swk(product(x[2 * tok :]).astype(BF16), 1).astype(F32)
            passed = (product(x[tok : 2 * tok]) + got[tok:]).astype(BF16)
            own = product(x[:tok]) + got[:tok]
            return [swk(passed[m * rows : (m + 1) * rows], 2) for m in range(micros)], passed, own

        d_before = (dot_t(after(cot, proj_term), w_proj) * slope.astype(F32)).astype(BF16)
        came, passed, own = reduce_quad(d_before, lambda x: dot_t(x, w_fc))
        d_normed2 = own + jnp.concatenate(came).astype(F32)
        fc_grad, fc_term = ffn_grad(after(normed2, passed), d_before)
        fc_b_grad = jnp.sum(d_before.astype(F32), axis=0)

        def across_quads(x, parts):
            size = x.shape[0] // parts
            outs = []
            for i in range(parts):
                block = x[i * size : (i + 1) * size]
                if i:
                    block = behind(block, outs[-1])
                for bit in bits_of(C)[2:]:
                    block = (block.astype(F32) + swk(block, bit).astype(F32)).astype(BF16)
                outs.append(block)
            return outs

        proj_sums = across_quads(proj_grad, 4)
        ffn, ffn_passed, ffn_own = reduce_quad(after(active, fc_term, came[0]), lambda x: dot(x, w_proj))

        d_middle, gain_two_grad, shift_two_grad = layer_norm_back(
            behind(middle, ffn_passed, ffn_own), gain_two, d_normed2
        )
        d_middle = cot_own.astype(F32) + d_middle
        d_branch = behind(d_middle, proj_sums[0]).astype(BF16)
        branch_own, branch_other = halves(d_branch)
        d_mixed = (dot_t(branch_own, wo_own) + dot_t(branch_other, wo_other)).astype(BF16)
        d_mixed = [d_mixed[m * rows : (m + 1) * rows] for m in range(micros)]
        kv_scale = jnp.concatenate([jnp.full((HD,), scale, F32), jnp.ones((HD,), F32)])
        d_queries = []
        kv_terms = []
        for m in range(micros):
            d_mixed[m] = behind(d_mixed[m], proj_sums[m + 1], *d_queries)
            dq, dkv = attend_backward(
                queries[m], d_mixed[m], mixed[m], lse[m], group_kv[m], kplace[m], qplace[m], scale
            )
            d_queries.append(dq)
            kv_terms.append(dkv)
        d_queries = jnp.concatenate(d_queries, axis=0)
        dq_own, dq_other = halves(behind(d_queries, proj_sums[3]))
        dq_pair = jnp.concatenate([dq_own, swk(dq_other, 1)], axis=0)
        normed1_pair = jnp.concatenate([normed1, swk(normed1, 1)], axis=0)
        query_term = t_dot(normed1_pair, dq_pair).astype(BF16)
        query_w_grad = scatter(query_term)
        branch_own, branch_other = halves(behind(d_branch, query_term))
        branch_pair = jnp.concatenate([branch_own, swk(branch_other, 1)], axis=0)
        mixed_pair = jnp.concatenate([all_mixed, swk(all_mixed, 1)], axis=0)
        out_term = t_dot(mixed_pair, branch_pair).astype(BF16)
        terms = jnp.stack(kv_terms) * behind(kv_scale, out_term)
        terms = terms.reshape(micros, C, rows, 2 * HD)
        terms = {d: terms[:, d] for d in range(C)}
        for bit in [1] + bits_of(C)[1:][::-1]:
            sent = [d for d in terms if d & bit]
            got = swk(jnp.stack([terms[d] for d in sent]).astype(BF16), bit)
            for i, d in enumerate(sent):
                terms[d ^ bit] = terms[d ^ bit] + got[i].astype(F32)
                del terms[d]
        d_keyvals = terms[0].astype(BF16).reshape(tok, 2 * HD)
        fc_came = swk(behind(fc_grad, d_keyvals), QUAD)
        dkv_own, dkv_other = halves(d_keyvals)
        dkv_pair = jnp.concatenate([dkv_own, swk(dkv_other, 1)], axis=0)
        keyval_term = t_dot(normed1_pair, dkv_pair).astype(BF16)
        out_w_grad = scatter(jnp.concatenate([out_term, keyval_term], axis=1))
        d_normed1 = (
            dot_t(d_queries, w_query) + dot_t(d_keyvals, w_keyval)
        )
        d_hidden, gain_one_grad, shift_one_grad = layer_norm_back(hidden, gain_one, d_normed1)
        hidden_grad = (d_middle + d_hidden).reshape(micros, rows, D)

        ffn = jnp.concatenate([behind(x, hidden_grad) for x in ffn]).astype(F32)
        result = middle + ffn_own + ffn + b_proj
        hidden_out = result.astype(BF16).reshape(micros, rows, D)

        fc_sum = (behind(fc_grad, hidden_grad, query_w_grad).astype(F32) + fc_came.astype(F32)).astype(BF16)
        for bit in bits_of(C)[3:]:
            fc_sum = (fc_sum.astype(F32) + swk(fc_sum, bit).astype(F32)).astype(BF16)

        def reduce_z(x):
            part = x.shape[0] // Z
            blocks = x.astype(BF16).reshape(Z, part, x.shape[1])
            terms = [
                lax.dynamic_slice(blocks, (zi ^ d, 0, 0), (1,) + blocks.shape[1:])[0].astype(F32)
                for d in range(Z)
            ]
            terms = dict(enumerate(terms))
            for bit in bits_of(Z):
                sent = [d for d in terms if d & bit]
                got = swk(jnp.concatenate([terms[d] for d in sent]).astype(BF16), 2 * bit)
                for i, d in enumerate(sent):
                    terms[d ^ bit] = terms[d ^ bit] + got[i * part : (i + 1) * part].astype(F32)
                    del terms[d]
            return terms[0].astype(BF16)

        def expand_z(held):
            part, n = held.shape
            ids = [0]
            for bit in bits_of(Z)[::-1]:
                held = jnp.concatenate([held, swk(held, 2 * bit)])
                ids = ids + [d ^ bit for d in ids]
            out = jnp.full((Z, part, n), 0.125, BF16)
            for i, d in enumerate(ids):
                block = held[i * part : (i + 1) * part]
                out = lax.dynamic_update_slice(out, block[None], (zi ^ d, 0, 0))
            own = out.reshape(Z * part, n)
            return own, swk(own, 1)

        query_block = reduce_z(query_w_grad)
        out_block = reduce_z(out_w_grad)

        members = (0, 2, 1, 3)
        proj_out = jnp.full((QUAD * width, D), 1.0, F32)
        for d, part in zip(members, gather_quad(behind(jnp.concatenate(proj_sums), d_keyvals))):
            proj_out = lax.dynamic_update_slice(proj_out, part.astype(F32), ((quad ^ d) * width, 0))
        fc_parts = jnp.full((QUAD, hsh, F * width), 0.75, BF16)
        fc_blocks = gather_quad(behind(fc_sum, query_block))
        for d, part in zip(members, fc_blocks):
            fc_parts = lax.dynamic_update_slice(fc_parts, part[None], (quad ^ d, 0, 0))
        fc_out = jnp.concatenate(
            [
                fc_parts[i][:, j * width : (j + 1) * width]
                for j in range(F)
                for i in range(QUAD)
            ],
            axis=1,
        ).astype(F32)
        query_out = in_order(*expand_z(query_block)).astype(F32)
        own, other = expand_z(out_block)
        half = D // 2
        out_out = in_order(own[:, :half], other[:, :half]).astype(F32)
        kv_sum = in_order(own[:, half:], other[:, half:]).astype(F32)

        fc_b_full = lax.dynamic_update_slice(
            jnp.zeros((F, QUAD, width), F32), fc_b_grad.reshape(F, 1, width), (0, quad, 0)
        )

        def sum_vectors(vectors):
            sizes = [v.size // F for v in vectors]
            packed = jnp.concatenate([v.reshape(F, -1) for v in vectors], axis=1)
            packed = jnp.pad(packed, ((0, 0), (0, -packed.shape[1] % 1024)))
            packed = packed.reshape(F, -1, 128)

            def one(d):
                return lax.dynamic_slice(packed, (f ^ d, 0, 0), (1,) + packed.shape[1:])[0]

            total = one(0)
            for d in range(1, F):
                total = total + swap_f(one(d), d, F)
            for bit in bits_of(C):
                total = total + swk(total, bit)
            total = total.reshape(-1)
            outs = []
            at = 0
            for size in sizes:
                outs.append(total[at : at + size])
                at += size
            return outs

        def column_sum(x):
            return jnp.sum(x.astype(F32), axis=0)

        g1, s1, bq, bv, g2, s2, bp, bo, bf = sum_vectors(
            [
                gain_one_grad,
                shift_one_grad,
                behind(column_sum(d_queries), fc_blocks[1]),
                column_sum(d_keyvals[:, HD:]),
                gain_two_grad,
                shift_two_grad,
                column_sum(cot_own),
                column_sum(d_branch),
                fc_b_full,
            ]
        )
        return (
            hidden_out, hidden_grad, g1, s1, query_out, bq, kv_sum, bv, out_out, bo, g2, s2,
            fc_out, bf, proj_out, bp,
        )

    return per_device


def solution(mesh):
    tokens = P(None, ("fsdp", "ctx"), None)
    places = P(None, ("fsdp", "ctx"))
    vec = P("fsdp")
    mat = P("fsdp", None)
    grads = (vec, vec, mat, vec, mat, vec, mat, vec, vec, vec, mat, vec, mat, vec)
    return jax.shard_map(
        build(mesh.shape["fsdp"], mesh.shape["ctx"]),
        mesh=mesh,
        in_specs=(tokens, places, places) + grads + (tokens,),
        out_specs=(tokens, tokens) + grads,
        check_vma=False,
    )
```

```python
import functools
import math

import jax
import jax.numpy as jnp
from jax import lax
from jax.experimental import pallas as pl
from jax.experimental.pallas import tpu as pltpu
from jax.sharding import PartitionSpec as P

D = 2048
HEADS = 16
HD = 128
QUAD = 4
F32 = jnp.float32
BF16 = jnp.bfloat16


def layer_norm(values, gain, shift):
    center = jnp.mean(values, axis=-1, keepdims=True)
    shifted = values - center
    spread = jnp.mean(shifted * shifted, axis=-1, keepdims=True)
    return shifted * lax.rsqrt(spread + 1e-05) * gain + shift


def layer_norm_back(values, gain, d_out):
    center = jnp.mean(values, axis=-1, keepdims=True)
    shifted = values - center
    spread = jnp.mean(shifted * shifted, axis=-1, keepdims=True)
    r = lax.rsqrt(spread + 1e-05)
    xhat = shifted * r
    e = d_out * gain
    d_values = r * (
        e - jnp.mean(e, axis=-1, keepdims=True) - xhat * jnp.mean(e * xhat, axis=-1, keepdims=True)
    )
    return d_values, jnp.sum(d_out * xhat, axis=0), jnp.sum(d_out, axis=0)


def gelu_and_slope(u):
    a = math.sqrt(2.0 / math.pi)
    t = jnp.tanh(a * (u + 0.044715 * u * u * u))
    half = 0.5 * (1.0 + t)
    slope = half + 0.5 * u * (1.0 - t * t) * a * (1.0 + 3.0 * 0.044715 * u * u)
    return u * half, slope


def dot(a, b):
    return jnp.dot(a, b, preferred_element_type=F32)


def dot_t(a, b):
    return lax.dot_general(a, b, (((1,), (1,)), ((), ())), preferred_element_type=F32)


def t_dot(a, b):
    return lax.dot_general(a, b, (((0,), (0,)), ((), ())), preferred_element_type=F32)


def swap_f(x, bit, size):
    return lax.ppermute(x, "fsdp", [(i, i ^ bit) for i in range(size)])


def swap_k(x, bit, size):
    return lax.ppermute(x, "ctx", [(i, i ^ bit) for i in range(size)])


def bits_of(size):
    out = []
    bit = 1
    while bit < size:
        out.append(bit)
        bit *= 2
    return out


def flip(index, d):
    bit = 1
    while bit <= d:
        if d & bit:
            index = index + bit * (1 - 2 * ((index // bit) % 2))
        bit *= 2
    return index


def head_kernel(
    F, C, vec_ref, place_ref, wkv_ref, wq_ref, vec_out, place_out, wkv_out, wq_out, send, recv, local
):
    f = lax.axis_index("fsdp")
    k = lax.axis_index("ctx")
    core = k % 2
    barrier = pltpu.get_barrier_semaphore()
    partners = [{"fsdp": flip(f, bit)} for bit in bits_of(F)]
    partners += [{"ctx": flip(k, bit)} for bit in bits_of(C)]
    for partner in partners:
        pl.semaphore_signal(barrier, inc=1, device_id=partner, device_id_type=pl.DeviceIdType.MESH)
    pl.semaphore_wait(barrier, len(partners))

    count = [0]
    started = []

    def remote(src, dst, partner):
        n = count[0]
        count[0] += 1
        copy = pltpu.make_async_remote_copy(
            src_ref=src,
            dst_ref=dst,
            send_sem=send.at[n],
            recv_sem=recv.at[n],
            device_id=partner,
            device_id_type=pl.DeviceIdType.MESH,
        )
        copy.start()
        started.append(copy)
        return copy

    own_copies = []

    def keep(src, dst):
        copy = pltpu.make_async_copy(src, dst, local.at[len(own_copies)])
        copy.start()
        own_copies.append(copy)

    def tree(own, place, order, me, axis, handed=None):
        come = {}

        def sends(d, position):
            for p in range(position, len(order)):
                src = own if d == 0 else place(d, d)
                copy = remote(src, place(d ^ order[p], d), {axis: flip(me, order[p])})
                come[d ^ order[p]] = (copy, p + 1)

        sends(0, 0)
        yield
        done = {0}
        while len(done) < len(come) + 1:
            for d in list(come):
                if d in done:
                    continue
                copy, position = come[d]
                copy.wait_recv()
                done.add(d)
                sends(d, position)
                if handed is not None:
                    handed(place(d, d))
                yield

    vec_rows = vec_ref.shape[0]
    trees = [
        tree(vec_ref, lambda d, e: vec_out.at[flip(f, e)], bits_of(F), f, "fsdp"),
    ]
    keep(vec_ref, vec_out.at[f])
    arrivals = []
    for ref, out in ((wkv_ref, wkv_out), (wq_ref, wq_out)):
        rows, width = ref.shape
        half, wide = rows // 2, width // 2
        columns = pl.ds(pl.multiple_of(core * wide, wide), wide)
        keep(ref, out.at[pl.ds(pl.multiple_of(f * rows, rows), rows)])
        for h, order in enumerate((bits_of(F), bits_of(F)[::-1])):

            def place(d, e, out=out, h=h, rows=rows, half=half, columns=columns):
                start = flip(f, e) * rows + h * half
                return out.at[pl.ds(pl.multiple_of(start, half), half), columns]

            def handed(block):
                arrivals.append(remote(block, block, {"ctx": flip(k, 1)}))

            own = ref.at[pl.ds(h * half, half), columns]
            trees.append(tree(own, place, order, f, "fsdp", handed))
    keep(place_ref, place_out.at[0])
    trees.append(tree(place_ref, lambda d, e: place_out.at[d], bits_of(C)[::-1], k, "ctx"))
    while trees:
        for one in list(trees):
            try:
                next(one)
            except StopIteration:
                trees.remove(one)
    for copy in arrivals:
        copy.wait_recv()
    for copy in started:
        copy.wait_send()
    for copy in own_copies:
        copy.wait()


def gather_head(F, C, vec, place, wkv, wq):
    copies = (F - 1) + (C - 1) + 2 * 2 * 2 * (F - 1)
    return pl.pallas_call(
        functools.partial(head_kernel, F, C),
        in_specs=[pl.BlockSpec(memory_space=pl.ANY)] * 4,
        out_specs=[pl.BlockSpec(memory_space=pl.ANY)] * 4,
        out_shape=[
            jax.ShapeDtypeStruct((F,) + vec.shape, vec.dtype),
            jax.ShapeDtypeStruct((C,) + place.shape, place.dtype),
            jax.ShapeDtypeStruct((F * wkv.shape[0], wkv.shape[1]), wkv.dtype),
            jax.ShapeDtypeStruct((F * wq.shape[0], wq.shape[1]), wq.dtype),
        ],
        scratch_shapes=[
            pltpu.SemaphoreType.DMA((copies,)),
            pltpu.SemaphoreType.DMA((copies,)),
            pltpu.SemaphoreType.DMA((4,)),
        ],
        compiler_params=pltpu.CompilerParams(collective_id=0, has_side_effects=True),
        name="gather_head",
    )(vec, place, wkv, wq)


HEAD_STEP = 4
KEY_STEP = 512


def forward_kernel(scale, q_ref, kv_ref, kplace_ref, qplace_ref, o_ref, lse_ref, bias, vt_ref, sc):
    keys = kv_ref.shape[0]

    @pl.when(pl.program_id(0) == 0)
    def _():
        fill_bias(kplace_ref, qplace_ref, bias)
        for at in range(0, keys, KEY_STEP):
            vt_ref[:, at : at + KEY_STEP] = kv_ref[at : at + KEY_STEP, HD:].T

    for h in range(HEAD_STEP):
        q = q_ref[:, h * HD : (h + 1) * HD]
        peak = None
        for at in range(0, keys, KEY_STEP):
            s = dot_t(kv_ref[at : at + KEY_STEP, :HD], q) * scale + bias[at : at + KEY_STEP]
            sc[h, at : at + KEY_STEP] = s
            top = jnp.max(s, axis=0, keepdims=True)
            peak = top if peak is None else jnp.maximum(peak, top)
        total = jnp.zeros_like(peak)
        acc = jnp.zeros((HD, q.shape[0]), F32)
        for at in range(0, keys, KEY_STEP):
            p = jnp.exp(sc[h, at : at + KEY_STEP] - peak)
            total = total + jnp.sum(p, axis=0, keepdims=True)
            acc = acc + dot(vt_ref[:, at : at + KEY_STEP], p.astype(BF16))
        o_ref[:, h * HD : (h + 1) * HD] = (acc / total).T.astype(BF16)
        lse_ref[0, h : h + 1] = peak + jnp.log(total)


def fill_bias(kplace_ref, qplace_ref, bias):
    for at in range(0, bias.shape[0], KEY_STEP):
        seg_k = kplace_ref[at : at + KEY_STEP, 0:1]
        pos_k = kplace_ref[at : at + KEY_STEP, 1:2]
        seg_q = qplace_ref[0:1]
        pos_q = qplace_ref[1:2]
        seen = (pos_k <= pos_q) & ((seg_k == 0) | (seg_k == seg_q))
        bias[at : at + KEY_STEP] = jnp.where(seen, 0.0, -1e30)


def backward_kernel(
    scale, q_ref, do_ref, o_ref, lse_ref, kv_ref, kplace_ref, qplace_ref, dq_ref, dkv_ref, bias, kt_ref
):
    keys = kv_ref.shape[0]

    @pl.when(pl.program_id(0) == 0)
    def _():
        fill_bias(kplace_ref, qplace_ref, bias)
        dkv_ref[...] = jnp.zeros_like(dkv_ref)
        for at in range(0, keys, KEY_STEP):
            kt_ref[:, at : at + KEY_STEP] = kv_ref[at : at + KEY_STEP, :HD].T

    for h in range(HEAD_STEP):
        q = q_ref[:, h * HD : (h + 1) * HD]
        do = do_ref[:, h * HD : (h + 1) * HD]
        o = o_ref[:, h * HD : (h + 1) * HD]
        inner = jnp.sum((do.astype(F32) * o.astype(F32)).T, axis=0, keepdims=True)
        lse = lse_ref[0, h : h + 1]
        dq = jnp.zeros((HD, q.shape[0]), F32)
        for at in range(0, keys, KEY_STEP):
            rows = slice(at, at + KEY_STEP)
            s = dot_t(kv_ref[rows, :HD], q) * scale + bias[rows]
            p = jnp.exp(s - lse)
            dp = dot_t(kv_ref[rows, HD:], do)
            ds = (p * (dp - inner)).astype(BF16)
            dkv_ref[rows, HD:] += dot(p.astype(BF16), do)
            dkv_ref[rows, :HD] += dot(ds, q)
            dq = dq + dot(kt_ref[:, rows], ds)
        dq_ref[:, h * HD : (h + 1) * HD] = (dq * scale).T.astype(BF16)


def attend_forward(queries, kv, kplace, qplace, scale):
    rows = queries.shape[0]
    keys = kv.shape[0]
    whole = lambda x: pl.BlockSpec(x.shape, lambda h: (0,) * x.ndim)
    heads = pl.BlockSpec((rows, HEAD_STEP * HD), lambda h: (0, h))
    return pl.pallas_call(
        functools.partial(forward_kernel, scale),
        grid=(HEADS // HEAD_STEP,),
        in_specs=[heads, whole(kv), whole(kplace), whole(qplace)],
        out_specs=[heads, pl.BlockSpec((1, HEAD_STEP, rows), lambda h: (h, 0, 0))],
        out_shape=[
            jax.ShapeDtypeStruct((rows, HEADS * HD), BF16),
            jax.ShapeDtypeStruct((HEADS // HEAD_STEP, HEAD_STEP, rows), F32),
        ],
        scratch_shapes=[
            pltpu.VMEM((keys, rows), F32),
            pltpu.VMEM((HD, keys), BF16),
            pltpu.VMEM((HEAD_STEP, keys, rows), F32),
        ],
        compiler_params=pltpu.CompilerParams(vmem_limit_bytes=32 * 1024 * 1024),
        cost_estimate=pl.CostEstimate(
            flops=8 * rows * keys * HEADS * HD,
            bytes_accessed=4 * rows * HEADS * HD,
            transcendentals=rows * keys * HEADS,
        ),
        name="attend_forward",
    )(queries, kv, kplace, qplace)


def attend_backward(queries, d_mixed, mixed, lse, kv, kplace, qplace, scale):
    rows = queries.shape[0]
    keys = kv.shape[0]
    whole = lambda x: pl.BlockSpec(x.shape, lambda h: (0,) * x.ndim)
    heads = pl.BlockSpec((rows, HEAD_STEP * HD), lambda h: (0, h))
    return pl.pallas_call(
        functools.partial(backward_kernel, scale),
        grid=(HEADS // HEAD_STEP,),
        in_specs=[
            heads,
            heads,
            heads,
            pl.BlockSpec((1, HEAD_STEP, rows), lambda h: (h, 0, 0)),
            whole(kv),
            whole(kplace),
            whole(qplace),
        ],
        out_specs=[heads, pl.BlockSpec((keys, 2 * HD), lambda h: (0, 0))],
        out_shape=[
            jax.ShapeDtypeStruct((rows, HEADS * HD), BF16),
            jax.ShapeDtypeStruct((keys, 2 * HD), F32),
        ],
        scratch_shapes=[pltpu.VMEM((keys, rows), F32), pltpu.VMEM((HD, keys), BF16)],
        compiler_params=pltpu.CompilerParams(vmem_limit_bytes=32 * 1024 * 1024),
        cost_estimate=pl.CostEstimate(
            flops=18 * rows * keys * HEADS * HD,
            bytes_accessed=8 * rows * HEADS * HD,
            transcendentals=rows * keys * HEADS,
        ),
        name="attend_backward",
    )(queries, d_mixed, mixed, lse, kv, kplace, qplace)


def build(F, C):
    Z = C // 2

    def per_device(
        hidden_in,
        segment_ids,
        positions,
        norm1_gain,
        norm1_bias,
        query_weight,
        query_bias,
        keyval_weight,
        value_bias,
        out_weight,
        out_bias,
        norm2_gain,
        norm2_bias,
        fc_weight,
        fc_bias,
        proj_weight,
        proj_bias,
        out_grad,
    ):
        micros, rows = hidden_in.shape[:2]
        tok = micros * rows
        scale = 1.0 / math.sqrt(HD)
        f = lax.axis_index("fsdp")
        k = lax.axis_index("ctx")
        core = k % 2
        quad = k % QUAD
        zi = k // 2
        hsh = D // F
        width = fc_weight.shape[1] // F // QUAD

        def pick_core(a, b):
            return jnp.where(core == 0, a, b)

        def in_order(own, other):
            return pick_core(
                jnp.concatenate([own, other], axis=1), jnp.concatenate([other, own], axis=1)
            )

        def halves(x):
            w = x.shape[1] // 2
            return pick_core(x[:, :w], x[:, w:]), pick_core(x[:, w:], x[:, :w])

        def after(x, *deps):
            return lax.optimization_barrier((x,) + deps)[0]

        def behind(x, *deps):
            zero = sum(
                jnp.minimum(jnp.abs(d[(slice(0, 1),) * d.ndim].reshape(()).astype(F32)), 0.0)
                for d in deps
            )
            return (x.astype(F32) + zero).astype(x.dtype)

        def swk(x, bit):
            return swap_k(x, bit, C)

        def gather_ctx(x):
            held = {0: x}
            for bit in bits_of(C)[1:][::-1] + [1]:
                for d in list(held):
                    held[d ^ bit] = swk(held[d], bit)
            return [held[d] for d in range(C)]

        def gather_quad(x):
            a = swk(x, 1)
            b = swk(x, 2)
            c = swk(b, 1)
            return [x, b, a, c]

        names = (
            norm1_gain, norm1_bias, query_bias, out_bias, norm2_gain, norm2_bias, proj_bias,
            fc_bias, value_bias,
        )
        sizes = [v.shape[0] for v in names]
        packed = jnp.concatenate(names)
        pad = -packed.shape[0] % 2048
        packed = jnp.pad(packed, (0, pad)).reshape(-1, 128)
        places = jnp.concatenate([segment_ids, positions], axis=0)
        vec, places, w_keyval, w_query = gather_head(
            F, C, packed, places, keyval_weight, query_weight
        )
        vec = vec.reshape(F, -1).astype(F32)
        full = []
        at = 0
        for size in sizes:
            full.append(vec[:, at : at + size])
            at += size
        gain_one, shift_one, b_query, b_out, gain_two, shift_two, b_proj = [
            v.reshape(-1) for v in full[:7]
        ]
        b_value = full[8].reshape(-1)
        b_fc = lax.dynamic_slice(
            full[7].reshape(F, QUAD, width), (0, quad, 0), (F, 1, width)
        ).reshape(-1)
        kv_bias = jnp.concatenate([jnp.zeros((HD,), F32), b_value])

        seg_all = [places[:, m].reshape(-1) for m in range(micros)]
        pos_all = [places[:, micros + m].reshape(-1) for m in range(micros)]

        wo_own = lax.all_gather(halves(out_weight)[0], "fsdp", axis=0, tiled=True)
        wo_other = swk(wo_own, 1)

        fc_piece = jnp.concatenate(
            [
                lax.dynamic_slice(fc_weight, (0, (j * QUAD + quad) * width), (hsh, width))
                for j in range(F)
            ],
            axis=1,
        )
        proj_piece = lax.dynamic_slice(proj_weight, (quad * width, 0), (width, D))
        w_fc = lax.all_gather(fc_piece, "fsdp", axis=0, tiled=True)
        w_proj = lax.all_gather(proj_piece, "fsdp", axis=0, tiled=True)

        hidden = hidden_in.reshape(tok, D).astype(F32)
        normed1 = layer_norm(hidden, gain_one, shift_one).astype(BF16)
        keyvals = (dot(normed1, w_keyval) + kv_bias).astype(BF16)
        group_kv = jnp.concatenate(
            gather_ctx(keyvals.reshape(micros, rows, 2 * HD)), axis=1
        )
        queries = (dot(normed1, w_query) + b_query).astype(BF16)
        kplace = [jnp.stack([seg_all[m], pos_all[m]], axis=1) for m in range(micros)]
        qplace = [jnp.stack([segment_ids[m], positions[m]]) for m in range(micros)]
        queries = [queries[m * rows : (m + 1) * rows] for m in range(micros)]
        mixed = []
        lse = []
        middle = []
        normed2_blocks = []
        for m in range(micros):
            mix, lse_rows = attend_forward(
                queries[m], group_kv[m], kplace[m], qplace[m], scale
            )
            mixed.append(mix)
            lse.append(lse_rows)
            mid = (
                hidden[m * rows : (m + 1) * rows]
                + in_order(dot(mix, wo_own), dot(mix, wo_other))
                + b_out
            )
            middle.append(mid)
            normed2_own = layer_norm(mid, gain_two, shift_two).astype(BF16)
            normed2_blocks.append(gather_quad(normed2_own))
            if m + 1 < micros:
                queries[m + 1] = behind(queries[m + 1], normed2_own)
        all_mixed = jnp.concatenate(mixed, axis=0)
        middle = jnp.concatenate(middle, axis=0)
        normed2 = jnp.concatenate(
            [normed2_blocks[m][d] for d in range(QUAD) for m in range(micros)], axis=0
        )
        cot_own = out_grad.reshape(tok, D)
        cot = jnp.concatenate(gather_quad(after(cot_own, group_kv)), axis=0)

        active, slope = gelu_and_slope(dot(normed2, w_fc) + b_fc)
        active = active.astype(BF16)
        slope = slope.astype(BF16)

        def scatter(term):
            return lax.psum_scatter(term, "fsdp", scatter_dimension=0, tiled=True)

        def ffn_grad(left, right):
            term = t_dot(left, right).astype(BF16)
            return lax.psum_scatter(term, "fsdp", scatter_dimension=0, tiled=True), term

        proj_grad, proj_term = ffn_grad(active, cot)

        def reduce_quad(x, product):
            got = swk(product(x[2 * tok :]).astype(BF16), 1).astype(F32)
            passed = (product(x[tok : 2 * tok]) + got[tok:]).astype(BF16)
            own = product(x[:tok]) + got[:tok]
            return [swk(passed[m * rows : (m + 1) * rows], 2) for m in range(micros)], passed, own

        d_before = (dot_t(cot, w_proj) * slope.astype(F32)).astype(BF16)
        came, passed, own = reduce_quad(d_before, lambda x: dot_t(x, w_fc))
        d_normed2 = own + jnp.concatenate(came).astype(F32)
        fc_grad, fc_term = ffn_grad(after(normed2, passed, proj_term), d_before)
        fc_b_grad = jnp.sum(d_before.astype(F32), axis=0)

        def across_quads(x, parts):
            size = x.shape[0] // parts
            outs = []
            for i in range(parts):
                block = x[i * size : (i + 1) * size]
                if i:
                    block = behind(block, outs[-1])
                for bit in bits_of(C)[2:]:
                    block = (block.astype(F32) + swk(block, bit).astype(F32)).astype(BF16)
                outs.append(block)
            return outs

        proj_sums = across_quads(proj_grad, 4)
        ffn, ffn_passed, ffn_own = reduce_quad(after(active, fc_term, came[0]), lambda x: dot(x, w_proj))

        d_middle, gain_two_grad, shift_two_grad = layer_norm_back(
            behind(middle, ffn_passed, ffn_own), gain_two, d_normed2
        )
        d_middle = cot_own.astype(F32) + d_middle
        d_branch = behind(d_middle, proj_sums[0]).astype(BF16)
        branch_own, branch_other = halves(d_branch)
        d_mixed = (dot_t(branch_own, wo_own) + dot_t(branch_other, wo_other)).astype(BF16)
        d_mixed = [d_mixed[m * rows : (m + 1) * rows] for m in range(micros)]
        kv_scale = jnp.concatenate([jnp.full((HD,), scale, F32), jnp.ones((HD,), F32)])
        d_queries = []
        kv_terms = []
        for m in range(micros):
            d_mixed[m] = behind(d_mixed[m], proj_sums[m + 1], *d_queries)
            dq, dkv = attend_backward(
                queries[m], d_mixed[m], mixed[m], lse[m], group_kv[m], kplace[m], qplace[m], scale
            )
            d_queries.append(dq)
            kv_terms.append(dkv)
        d_queries = jnp.concatenate(d_queries, axis=0)
        dq_own, dq_other = halves(behind(d_queries, proj_sums[3]))
        dq_pair = jnp.concatenate([dq_own, swk(dq_other, 1)], axis=0)
        normed1_pair = jnp.concatenate([normed1, swk(normed1, 1)], axis=0)
        query_term = t_dot(normed1_pair, dq_pair).astype(BF16)
        query_w_grad = scatter(query_term)
        branch_own, branch_other = halves(behind(d_branch, query_term))
        branch_pair = jnp.concatenate([branch_own, swk(branch_other, 1)], axis=0)
        mixed_pair = jnp.concatenate([all_mixed, swk(all_mixed, 1)], axis=0)
        out_term = t_dot(mixed_pair, branch_pair).astype(BF16)
        terms = jnp.stack(kv_terms) * behind(kv_scale, out_term)
        terms = terms.reshape(micros, C, rows, 2 * HD)
        terms = {d: terms[:, d] for d in range(C)}
        for bit in [1] + bits_of(C)[1:][::-1]:
            sent = [d for d in terms if d & bit]
            got = swk(jnp.stack([terms[d] for d in sent]).astype(BF16), bit)
            for i, d in enumerate(sent):
                terms[d ^ bit] = terms[d ^ bit] + got[i].astype(F32)
                del terms[d]
        d_keyvals = terms[0].astype(BF16).reshape(tok, 2 * HD)
        fc_came = swk(behind(fc_grad, d_keyvals), QUAD)
        dkv_own, dkv_other = halves(d_keyvals)
        dkv_pair = jnp.concatenate([dkv_own, swk(dkv_other, 1)], axis=0)
        keyval_term = t_dot(normed1_pair, dkv_pair).astype(BF16)
        out_w_grad = scatter(jnp.concatenate([out_term, keyval_term], axis=1))
        d_normed1 = (
            dot_t(d_queries, w_query) + dot_t(d_keyvals, w_keyval)
        )
        d_hidden, gain_one_grad, shift_one_grad = layer_norm_back(hidden, gain_one, d_normed1)
        hidden_grad = (d_middle + d_hidden).reshape(micros, rows, D)

        ffn = jnp.concatenate([behind(x, hidden_grad) for x in ffn]).astype(F32)
        result = middle + ffn_own + ffn + b_proj
        hidden_out = result.astype(BF16).reshape(micros, rows, D)

        fc_sum = (behind(fc_grad, hidden_grad, query_w_grad).astype(F32) + fc_came.astype(F32)).astype(BF16)
        for bit in bits_of(C)[3:]:
            fc_sum = (fc_sum.astype(F32) + swk(fc_sum, bit).astype(F32)).astype(BF16)

        def reduce_z(x):
            part = x.shape[0] // Z
            blocks = x.astype(BF16).reshape(Z, part, x.shape[1])
            terms = [
                lax.dynamic_slice(blocks, (zi ^ d, 0, 0), (1,) + blocks.shape[1:])[0].astype(F32)
                for d in range(Z)
            ]
            terms = dict(enumerate(terms))
            for bit in bits_of(Z):
                sent = [d for d in terms if d & bit]
                got = swk(jnp.concatenate([terms[d] for d in sent]).astype(BF16), 2 * bit)
                for i, d in enumerate(sent):
                    terms[d ^ bit] = terms[d ^ bit] + got[i * part : (i + 1) * part].astype(F32)
                    del terms[d]
            return terms[0].astype(BF16)

        def expand_z(held):
            part, n = held.shape
            ids = [0]
            for bit in bits_of(Z)[::-1]:
                held = jnp.concatenate([held, swk(held, 2 * bit)])
                ids = ids + [d ^ bit for d in ids]
            out = jnp.full((Z, part, n), 0.125, BF16)
            for i, d in enumerate(ids):
                block = held[i * part : (i + 1) * part]
                out = lax.dynamic_update_slice(out, block[None], (zi ^ d, 0, 0))
            own = out.reshape(Z * part, n)
            return own, swk(own, 1)

        query_block = reduce_z(query_w_grad)
        out_block = reduce_z(out_w_grad)

        members = (0, 2, 1, 3)
        proj_out = jnp.full((QUAD * width, D), 1.0, F32)
        for d, part in zip(members, gather_quad(behind(jnp.concatenate(proj_sums), d_keyvals))):
            proj_out = lax.dynamic_update_slice(proj_out, part.astype(F32), ((quad ^ d) * width, 0))
        fc_parts = jnp.full((QUAD, hsh, F * width), 0.75, BF16)
        fc_blocks = gather_quad(behind(fc_sum, query_block))
        for d, part in zip(members, fc_blocks):
            fc_parts = lax.dynamic_update_slice(fc_parts, part[None], (quad ^ d, 0, 0))
        fc_out = jnp.concatenate(
            [
                fc_parts[i][:, j * width : (j + 1) * width]
                for j in range(F)
                for i in range(QUAD)
            ],
            axis=1,
        ).astype(F32)
        query_out = in_order(*expand_z(query_block)).astype(F32)
        own, other = expand_z(out_block)
        half = D // 2
        out_out = in_order(own[:, :half], other[:, :half]).astype(F32)
        kv_sum = in_order(own[:, half:], other[:, half:]).astype(F32)

        fc_b_full = lax.dynamic_update_slice(
            jnp.zeros((F, QUAD, width), F32), fc_b_grad.reshape(F, 1, width), (0, quad, 0)
        )

        def sum_vectors(vectors):
            sizes = [v.size // F for v in vectors]
            packed = jnp.concatenate([v.reshape(F, -1) for v in vectors], axis=1)
            packed = jnp.pad(packed, ((0, 0), (0, -packed.shape[1] % 1024)))
            packed = packed.reshape(F, -1, 128)

            def one(d):
                return lax.dynamic_slice(packed, (f ^ d, 0, 0), (1,) + packed.shape[1:])[0]

            total = one(0)
            for d in range(1, F):
                total = total + swap_f(one(d), d, F)
            for bit in bits_of(C):
                total = total + swk(total, bit)
            total = total.reshape(-1)
            outs = []
            at = 0
            for size in sizes:
                outs.append(total[at : at + size])
                at += size
            return outs

        def column_sum(x):
            return jnp.sum(x.astype(F32), axis=0)

        g1, s1, bq, bv, g2, s2, bp, bo, bf = sum_vectors(
            [
                gain_one_grad,
                shift_one_grad,
                behind(column_sum(d_queries), fc_blocks[1]),
                column_sum(d_keyvals[:, HD:]),
                gain_two_grad,
                shift_two_grad,
                column_sum(cot_own),
                column_sum(d_branch),
                fc_b_full,
            ]
        )
        return (
            hidden_out, hidden_grad, g1, s1, query_out, bq, kv_sum, bv, out_out, bo, g2, s2,
            fc_out, bf, proj_out, bp,
        )

    return per_device


def solution(mesh):
    tokens = P(None, ("fsdp", "ctx"), None)
    places = P(None, ("fsdp", "ctx"))
    vec = P("fsdp")
    mat = P("fsdp", None)
    grads = (vec, vec, mat, vec, mat, vec, mat, vec, vec, vec, mat, vec, mat, vec)
    return jax.shard_map(
        build(mesh.shape["fsdp"], mesh.shape["ctx"]),
        mesh=mesh,
        in_specs=(tokens, places, places) + grads + (tokens,),
        out_specs=(tokens, tokens) + grads,
        check_vma=False,
    )
```
